512 devices in a mesh: tm: 64 (over x, y, core), lat: 8 (over z).
Axes of the slice: x: 4, y: 8, z: 8, core: 2. Of those that a mesh axis runs over, the one named last changes fastest.
Arguments:
- x_init: float32 [64, 5, 64, 1024], P('tm', None, 'lat'), may hold values from -6 to 6
- background: float32 [5, 64, 1024], P(None, 'lat'), may hold values from -6 to 6
- observed: float32 [64, 64, 1024], P('tm', 'lat'), may hold values from -6 to 6
- diff_lon: float32 [64, 64, 1024], P('tm', 'lat'), may hold values from 0.03 to 0.2
- diff_lat: float32 [64, 64, 1024], P('tm', 'lat'), may hold values from 0.03 to 0.2
- drift: float32 [64, 64, 1024], P('tm', 'lat'), may hold values from -0.3 to 0.3
- coupling: float32 [5, 5], replicated, may hold values from -0.4 to 0.4
- model_var: float32 [5], replicated, may hold values from 0.3 to 3
- obs_level: int32 [64, 64, 8], P('tm', 'lat'), may hold values from 0 to 4
- huber_class: int32 [64, 64, 8], P('tm', 'lat'), may hold values from 0 to 2
Outputs:
- state: float32 [64, 5, 64, 1024], P('tm', None, 'lat')
- multipliers: float32 [64, 5, 64, 1024], P('tm', None, 'lat')
- obs_multipliers: float32 [64, 64, 1024], P('tm', 'lat')
The draws below stay inside these ranges and needn't reach their ends.
All inputs are finite; a program needn't handle non-finite values.
Results may differ from the reference program's by a relative error of at most 0.0003.
Values sent between devices are 32-bit elements; how exact they have to be, the bound alone decides.
No kernel may reach another device: no remote copies, remote signals or barrier semaphores. Data moves between devices by JAX's collectives and lax.ppermute only.
A program may use at most 64 MiB of HBM per device.

```python
import math
import jax
import jax.numpy as jnp
from jax import lax

LEVELS = 5
LONC = 1024
TILE = 128
STEPS = 4
ITERS = 2
NT = 64
NLAT = 64
NTILE = 8


def plant(result, own_key, low, top_value):
    longest = result.shape.index(max(result.shape))
    spots = []
    for shift in (0, 1):
        where = [jax.random.randint(jax.random.fold_in(own_key, axis), (), 0, length) for axis, length in enumerate(result.shape)]
        where[longest] = (where[longest] + shift) % result.shape[longest]
        spots.append(tuple(where))
    return result.at[spots[0]].set(low).at[spots[1]].set(top_value)


def block_levels(rng, extent, shards, low, high):
    def one(position, shards_of):
        draws = jax.random.uniform(jax.random.fold_in(jax.random.fold_in(rng, 6), position), (shards_of,), jnp.float32, low / len(shards), high / len(shards))
        return jnp.repeat(jnp.exp(draws), extent[position] // shards_of).reshape((-1,) + (1,) * (len(extent) - position - 1))

    loudness = one(*shards[0])
    for cut in shards[1:]:
        loudness = loudness * one(*cut)
    return loudness


def bell_draw(key, extent, scale, reach, cuts=(), kind=jnp.bfloat16):
    drawn = jax.random.normal(key, extent, jnp.float32) * scale
    if len(cuts) > 0:
        drawn = block_levels(key, extent, cuts, -0.22, 0.18) * drawn
    return jnp.clip(drawn, min=-reach, max=reach).astype(kind)


def setup_inputs(seed: int = 0) -> dict:
    streams_of = jax.random.split(jax.random.key(seed), 11)
    return {
        "x_init": bell_draw(streams_of[0], (NT, LEVELS, NLAT, LONC), 1.0, 6.0, ((0, 64), (2, 8)), jnp.float32),
        "background": bell_draw(streams_of[1], (LEVELS, NLAT, LONC), 1.0, 6.0, ((1, 8),), jnp.float32),
        "observed": bell_draw(streams_of[2], (NT, NLAT, LONC), 1.0, 6.0, ((0, 64), (1, 8)), jnp.float32),
        "diff_lon": jnp.clip(0.03 + 0.17 * jax.random.uniform(streams_of[3], (NT, NLAT, LONC), jnp.float32) ** block_levels(streams_of[3], (NT, NLAT, LONC), ((0, 64), (1, 8)), -0.2, 0.2), 0.03, 0.2),
        "diff_lat": jnp.clip(0.03 + 0.17 * jax.random.uniform(streams_of[4], (NT, NLAT, LONC), jnp.float32) ** block_levels(streams_of[4], (NT, NLAT, LONC), ((0, 64), (1, 8)), -0.2, 0.2), 0.03, 0.2),
        "drift": jnp.clip(jax.random.uniform(streams_of[5], (NT, NLAT, LONC), jnp.float32, -0.3, 0.3) * block_levels(streams_of[5], (NT, NLAT, LONC), ((0, 64), (1, 8)), -0.4, 0.0), -0.3, 0.3),
        "coupling": bell_draw(streams_of[6], (LEVELS, LEVELS), 0.1, 0.4, (), jnp.float32),
        "model_var": jnp.clip(jnp.exp(jax.random.uniform(streams_of[7], (LEVELS,), jnp.float32, math.log(0.3), math.log(3.0))), 0.3, 3.0),
        "obs_level": plant(jax.random.randint(streams_of[8], (NT, NLAT, NTILE), 0, LEVELS), jax.random.fold_in(streams_of[8], 1), 0, LEVELS - 1).astype(jnp.int32),
        "huber_class": plant(jax.random.randint(streams_of[9], (NT, NLAT, NTILE), 0, 3), jax.random.fold_in(streams_of[9], 1), 0, 2).astype(jnp.int32),
    }


def local_step(v, north, south, kx, ky, ux, coupling):
    east = jnp.roll(v, -1, 2)
    west = jnp.roll(v, 1, 2)
    mixed = jnp.einsum('lm,mrc->lrc', coupling, v, precision=lax.Precision.HIGHEST)
    return v + kx * (east + west - 2.0 * v) + ky * (north + south - 2.0 * v) + 0.5 * ux * (east - west) + mixed

def adjoint_local(w, qnorth, qsouth, kx, ky, ux, coupling):
    p_term = kx * w
    q_term = ky * w
    u_term = ux * w
    mixed = jnp.einsum('lm,lrc->mrc', coupling, w, precision=lax.Precision.HIGHEST)
    lon_part = jnp.roll(p_term, -1, 2) + jnp.roll(p_term, 1, 2) - 2.0 * p_term
    adv_part = 0.5 * (jnp.roll(u_term, 1, 2) - jnp.roll(u_term, -1, 2))
    return w + lon_part + qnorth + qsouth - 2.0 * q_term + adv_part + mixed

def forward_model(v, kx, ky, ux, coupling):
    for step in range(STEPS):
        padded = jnp.pad(v, ((0, 0), (1, 1), (0, 0)))
        v = local_step(v, padded[:, 2:], padded[:, :-2], kx, ky, ux, coupling)
    return v

def adjoint_model(w, kx, ky, ux, coupling):
    for step in range(STEPS):
        padded = jnp.pad(ky * w, ((0, 0), (1, 1), (0, 0)))
        w = adjoint_local(w, padded[:, 2:], padded[:, :-2], kx, ky, ux, coupling)
    return w

def level_table(obs_level):
    levels = jnp.arange(LEVELS, dtype=jnp.int32)
    return (obs_level[None] == levels[:, None, None]).astype(jnp.float32)

def sample(x, table):
    lev, rows, cols = x.shape
    pieces = x.reshape(lev, rows, cols // TILE, TILE) * table[..., None]
    return lax.optimization_barrier(jnp.sum(pieces, axis=0)).reshape(rows, cols)

def spread(field, table):
    rows, cols = field.shape
    pieces = table[..., None] * field.reshape(rows, cols // TILE, TILE)[None]
    return pieces.reshape(table.shape[0], rows, cols)

def huber_cells(huber_class):
    tiles = 1.0 * (huber_class == 0) + 0.5 * (huber_class == 1) + 0.25 * (huber_class == 2)
    tiles = tiles.astype(jnp.float32)
    rows, count = tiles.shape
    return (tiles[..., None] * jnp.ones((TILE,), jnp.float32)).reshape(rows, count * TILE)

def reference(x_init, background, observed, diff_lon, diff_lat, drift, coupling, model_var, obs_level, huber_class):
    tables = jax.vmap(level_table)(obs_level)
    weights = jax.vmap(huber_cells)(huber_class)
    run_forward = jax.vmap(forward_model, in_axes=(0, 0, 0, 0, None))
    run_adjoint = jax.vmap(adjoint_model, in_axes=(0, 0, 0, 0, None))
    state = x_init
    multipliers = jnp.zeros_like(x_init)
    obs_multipliers = jnp.zeros_like(observed)
    for it in range(ITERS):
        moved = run_forward(state, diff_lon, diff_lat, drift, coupling)
        prior = jnp.concatenate([background[None], moved[:-1]], axis=0)
        multipliers = multipliers + 0.5 * (state - prior - model_var[None, :, None, None] * multipliers)
        misfit = jax.vmap(sample)(state, tables) - observed
        obs_multipliers = obs_multipliers + 0.5 * (weights * misfit - obs_multipliers)
        later = jnp.concatenate([multipliers[1:], jnp.zeros_like(multipliers[:1])], axis=0)
        pulled = run_adjoint(later, diff_lon, diff_lat, drift, coupling)
        gradient = multipliers - pulled + jax.vmap(spread)(obs_multipliers, tables)
        scale = jnp.sqrt(jnp.sum(gradient * gradient) / gradient.size + 1e-06)
        state = state - 0.3 * gradient / scale
    return (state, multipliers, obs_multipliers)
```

```python
import jax
import jax.numpy as jnp
from jax import lax
from jax.experimental import pallas as pl
from jax.experimental.pallas import tpu as pltpu
from jax.sharding import Mesh
from jax.sharding import PartitionSpec as P

L = 5
TILE = 128
STEPS = 4
ROWS = 8
H = STEPS
W = ROWS + 2 * H
TM = ("tm_0", "tm_1", "tm_2")
FAR = ("tm_0", "tm_1")
NEAR = ("tm_2", "lat")
ROW = (8, TILE)


def lanes():
    return lax.broadcasted_iota(jnp.int32, ROW, 1)


class Shift:
    def __init__(self):
        lane = lanes()
        self.first = lane == 0
        self.last = lane == TILE - 1

    def east(self, v):
        r = pltpu.roll(v, TILE - 1, 1)
        return jnp.where(self.last, pltpu.roll(r, 7, 0), r)

    def west(self, v):
        r = pltpu.roll(v, 1, 1)
        return jnp.where(self.first, pltpu.roll(r, 1, 0), r)


def total(terms):
    while len(terms) > 1:
        terms = [a + b for a, b in zip(terms[::2], terms[1::2])] + (
            [terms[-1]] if len(terms) % 2 else []
        )
    return terms[0]


def centre(ce, cw, ky):
    return (1.0 - (ce + cw)) - 2.0 * ky


def forward(src, coef, c, rows, bufs, dst):
    sh = Shift()
    for step in range(STEPS):
        lo, hi = step + 1, rows - step - 1

        def get(r, step=step):
            if step == 0:
                return [src(l, r) for l in range(L)]
            return [bufs[(step - 1) % 2][l, r] for l in range(L)]

        above, here = get(lo - 1), get(lo)
        for r in range(lo, hi):
            below = get(r + 1)
            ce, cw, ky = coef(0, r), coef(1, r), coef(2, r)
            c0 = centre(ce, cw, ky)
            for l in range(L):
                v = here[l]
                terms = [
                    ce * sh.east(v),
                    cw * sh.west(v),
                    ky * (above[l] + below[l]),
                    c0 * v,
                ] + [c[l][m] * here[m] for m in range(L)]
                out = total(terms)
                if step == STEPS - 1:
                    dst(l, r, out)
                else:
                    bufs[step % 2][l, r] = out
            above, here = here, below


def adjoint(src, coef, c, rows, bufs, dst):
    sh = Shift()
    for step in range(STEPS):
        lo, hi = step + 1, rows - step - 1

        def get(r, step=step):
            if step == 0:
                v = [src(l, r) for l in range(L)]
            else:
                v = [bufs[(step - 1) % 2][l, r] for l in range(L)]
            ky = coef(2, r)
            return v, [ky * w for w in v]

        (_, above), (here, q) = get(lo - 1), get(lo)
        for r in range(lo, hi):
            after, below = get(r + 1)
            ce, cw, ky = coef(0, r), coef(1, r), coef(2, r)
            c0 = centre(ce, cw, ky)
            for l in range(L):
                w = here[l]
                terms = [
                    sh.west(ce * w),
                    sh.east(cw * w),
                    above[l] + below[l],
                    c0 * w,
                ] + [c[m][l] * here[m] for m in range(L)]
                out = total(terms)
                if step == STEPS - 1:
                    dst(l, r, out)
                else:
                    bufs[step % 2][l, r] = out
            above, here, q = q, after, below


def scalars(ref):
    return [[ref[l, m] for m in range(L)] for l in range(L)]


def banded(up, own, down, first):
    def at(k, r):
        part = (up, own, down)[r // ROWS]
        return part[first + k, r % ROWS]

    return at


def not_last():
    j = (lax.axis_index("tm_0") * lax.axis_size("tm_1") + lax.axis_index("tm_1")) * lax.axis_size(
        "tm_2"
    ) + lax.axis_index("tm_2")
    last = lax.axis_size("tm_0") * lax.axis_size("tm_1") * lax.axis_size("tm_2") - 1
    return jnp.where(j == last, 0.0, 1.0), jnp.where(j == 0, 1.0, 0.0)


def split(v):
    return jnp.swapaxes(jnp.stack([v[:, s * TILE : (s + 1) * TILE] for s in range(8)]), 0, 1)


def join_into(ref, index, rows):
    v = jnp.swapaxes(jnp.stack(rows), 0, 1)
    for s in range(8):
        ref[(*index, slice(None), slice(s * TILE, (s + 1) * TILE))] = v[s]


def pack_kernel(x, kx, ky, ux, out):
    for l in range(L):
        out[l] = split(x[l])
    k, u = kx[...], 0.5 * ux[...]
    out[L] = split(k + u)
    out[L + 1] = split(k - u)
    out[L + 2] = split(ky[...])


def aside_kernel(background, observed, bg, obs):
    for l in range(L):
        bg[l] = split(background[l])
    obs[...] = split(observed[...])


def middle_kernel(up, own, down, all_out, x_out):
    for k in range(L + 3):
        for ref, rows, base in ((up, range(H, ROWS), 0), (own, range(ROWS), H), (down, range(H), H + ROWS)):
            for r in rows:
                v = ref[k, r]
                to = base + r - (H if base == 0 else 0)
                all_out[k, to] = v
                if k < L:
                    x_out[k, to] = v


def middle_g_kernel(up, own, down, out):
    for k in range(L):
        out[k, :H] = up[k, H:]
        out[k, H : H + ROWS] = own[k]
        out[k, H + ROWS :] = down[k, :H]


def forward_kernel(c_ref, up, own, down, up_c, own_c, down_c, out, a, b):
    def dst(l, r, v):
        out[l, r - H] = v

    forward(
        banded(up, own, down, 0),
        banded(up_c, own_c, down_c, L),
        scalars(c_ref),
        3 * ROWS,
        (a, b),
        dst,
    )


def picked(level, values):
    out = jnp.zeros(ROW, jnp.float32)
    for l in range(L):
        out = out + jnp.where(level == l, values[l], 0.0)
    return out


def gradient_kernel(
    c_ref, before, after, moved, up, own, down, bg, obs, level, weight, g, d, ahead, o1, a, b
):
    c = scalars(c_ref)
    some, first = not_last()
    half = 0.5 * some
    for l in range(L):
        for r in range(W):
            ahead[l, r] = half * (after[l, r] - moved[l, r])

    def prior(l, r, v):
        d[l, r - H] = 0.5 * (own[l, r - H] - (v + first * bg[l, r - H]))

    forward(lambda l, r: before[l, r], lambda k, r: before[L + k, r], c, W, (a, b), prior)
    coef = banded(up, own, down, L)
    for r in range(ROWS):
        o1[r] = 0.5 * weight[r] * (picked(level[r], [own[l, r] for l in range(L)]) - obs[r])

    def dst(l, r, v):
        r = r - H
        g[l, r] = d[l, r] - v + jnp.where(level[r] == l, o1[r], 0.0)

    adjoint(lambda l, r: ahead[l, r], lambda k, r: coef(k, r + H), c, W, (a, b), dst)


def still_kernel(c_ref, var, d, ahead, own, up, down, level, o1, g0, a, b):
    c = scalars(c_ref)
    keep = [2.0 - 0.5 * var[l] for l in range(L)]
    coef = banded(up, own, down, L)

    def dst(l, r, v):
        r = r - H
        g0[l, r] = keep[l] * d[l, r] - v + jnp.where(level[r] == l, 1.5 * o1[r], 0.0)

    adjoint(lambda l, r: keep[l] * ahead[l, r], lambda k, r: coef(k, r + H), c, W, (a, b), dst)


def curvature_kernel(
    c_ref, coefs, before, after, moved, up, own, down, own_g, level, weight, g0, u, g1, hg, part, ahead, a, b
):
    c = scalars(c_ref)
    some, _ = not_last()
    for l in range(L):
        for r in range(W):
            ahead[l, r] = some * (after[l, r] - moved[l, r])

    def misfit(l, r, v):
        u[l, r - H] = own_g[l, r - H] - v

    forward(lambda l, r: before[l, r], lambda k, r: coefs[L + k, r], c, W, (a, b), misfit)
    coef = banded(up, own, down, L)
    for r in range(ROWS):
        hg[r] = weight[r] * picked(level[r], [own_g[l, r] for l in range(L)])
    sums = [[], [], [], []]

    def dst(l, r, v):
        r = r - H
        one = -0.5 * (u[l, r] - v + jnp.where(level[r] == l, hg[r], 0.0))
        g1[l, r] = one
        zero, first = g0[l, r], own_g[l, r]
        for k, term in enumerate((first * first, zero * zero, zero * one, one * one)):
            sums[k].append(term)
            if len(sums[k]) == 5:
                sums[k] = [total(sums[k])]

    adjoint(lambda l, r: ahead[l, r], lambda k, r: coef(k, r + H), c, W, (a, b), dst)
    lane = lax.broadcasted_iota(jnp.int32, (1, TILE), 1)
    row = jnp.zeros((1, TILE), jnp.float32)
    for k in range(4):
        s = jnp.sum(total(sums[k]))
        row = jnp.where(lane == k, s, row)
    for i in range(part.shape[0]):
        part[i] = row


def again_kernel(parts, out):
    s = total([parts[i] for i in range(parts.shape[0])])
    for i in range(out.shape[0]):
        out[i] = s


def last_kernel(count, parts, var, own, g, g0, g1, d, u, o1, hg, state, multipliers, obs):
    row = total([parts[i] for i in range(parts.shape[0])])
    lane = lax.broadcasted_iota(jnp.int32, (1, TILE), 1)
    sg, s00, s01, s11 = [
        jnp.broadcast_to(jnp.sum(jnp.where(lane == k, row, 0.0), axis=1, keepdims=True), ROW) / count
        for k in range(4)
    ]
    first = 0.3 / jnp.sqrt(sg + 1e-06)
    mean = jnp.maximum(s00 + first * (2.0 * s01 + first * s11), 0.0)
    second = 0.3 / jnp.sqrt(mean + 1e-06)
    for l in range(L):
        keep = 2.0 - 0.5 * var[l]
        join_into(
            state,
            (l,),
            [
                own[l, r] - first * g[l, r] - second * (g0[l, r] + first * g1[l, r])
                for r in range(ROWS)
            ],
        )
        join_into(multipliers, (l,), [keep * d[l, r] - (0.5 * first) * u[l, r] for r in range(ROWS)])
    join_into(obs, (), [1.5 * o1[r] - (0.5 * first) * hg[r] for r in range(ROWS)])


VM = pl.BlockSpec(memory_space=pltpu.VMEM)
SM = pl.BlockSpec(memory_space=pltpu.SMEM)


def call(kernel, outs, smem=0, scratch=(), us=1.0):
    def run(*args):
        n = sum(a.size for a in args)
        return pl.pallas_call(
            kernel,
            out_shape=[jax.ShapeDtypeStruct(s, jnp.float32) for s in outs],
            in_specs=[SM] * smem + [VM] * (len(args) - smem),
            out_specs=[VM] * len(outs),
            scratch_shapes=[pltpu.VMEM(s, jnp.float32) for s in scratch],
            compiler_params=pltpu.CompilerParams(vmem_limit_bytes=16 * 2**20),
            cost_estimate=pl.CostEstimate(flops=int(us * 4e6), bytes_accessed=4 * n, transcendentals=0),
        )(*args)

    return run


def rows_of(k, n):
    return (k, n, *ROW)


def shifted(x, axis, by):
    count = lax.axis_size(axis)
    return lax.ppermute(x, axis, [(i, i + by) for i in range(count) if 0 <= i + by < count])


def exchanged(x, axis):
    return lax.all_to_all(x, axis, 0, 0, tiled=True)


def on_device(
    x_init, background, observed, diff_lon, diff_lat, drift, coupling, model_var, obs_level, huber_class
):
    count = float(
        L * ROWS * 8 * TILE * lax.axis_size(TM) * lax.axis_size("lat")
    )
    two = [rows_of(L, 3 * ROWS)] * 2
    two_w = [rows_of(L, W)] * 2
    (own,) = call(pack_kernel, [rows_of(L + 3, ROWS)])(x_init[0], diff_lon[0], diff_lat[0], drift[0])
    up, down = shifted(own, "lat", 1), shifted(own, "lat", -1)
    bg, obs = call(aside_kernel, [rows_of(L, ROWS), (ROWS, *ROW)])(background, observed[0])
    level = jnp.broadcast_to(obs_level[0][..., None], (ROWS, *ROW))
    classes = huber_class[0]
    weight = 1.0 * (classes == 0) + 0.5 * (classes == 1) + 0.25 * (classes == 2)
    weight = jnp.broadcast_to(weight.astype(jnp.float32)[..., None], (ROWS, *ROW))

    wide, wide_x = call(middle_kernel, [rows_of(L + 3, W), rows_of(L, W)])(up, own, down)
    before, after = shifted(wide, TM, 1), shifted(wide_x, TM, -1)
    (moved,) = call(forward_kernel, [rows_of(L, W)], 1, two, 2.0)(
        coupling, up, own, down, up, own, down
    )
    g, d, ahead, o1 = call(
        gradient_kernel,
        [rows_of(L, ROWS), rows_of(L, ROWS), rows_of(L, W), (ROWS, *ROW)],
        1,
        two_w,
        3.0,
    )(coupling, before, after, moved, up, own, down, bg, obs, level, weight)

    up_g, down_g = shifted(g, "lat", 1), shifted(g, "lat", -1)
    (g0,) = call(still_kernel, [rows_of(L, ROWS)], 2, two_w, 2.0)(
        coupling, model_var, d, ahead, own, up, down, level, o1
    )
    (wide_g,) = call(middle_g_kernel, [rows_of(L, W)])(up_g, g, down_g)
    before_g, after_g = shifted(wide_g, TM, 1), shifted(wide_g, TM, -1)
    (moved_g,) = call(forward_kernel, [rows_of(L, W)], 1, two, 2.0)(
        coupling, up_g, g, down_g, up, own, down
    )
    u, g1, hg, part = call(
        curvature_kernel,
        [rows_of(L, ROWS), rows_of(L, ROWS), (ROWS, *ROW), (lax.axis_size(NEAR), 1, TILE)],
        1,
        [rows_of(L, W)] + two_w,
        3.0,
    )(coupling, before, before_g, after_g, moved_g, up, own, down, g, level, weight, g0)
    (part,) = call(again_kernel, [(lax.axis_size(FAR), 1, TILE)])(exchanged(part, NEAR))
    part = exchanged(part, FAR)

    natural = (L, ROWS, 8 * TILE)

    def finish(var, part, *refs):
        last_kernel(count, part, var, *refs)

    state, multipliers, obs_multipliers = call(finish, [natural, natural, natural[1:]], 1)(
        model_var, part, own, g, g0, g1, d, u, o1, hg
    )
    return (state[None], multipliers[None], obs_multipliers[None])


def solution(mesh):
    torus = Mesh(mesh.devices.reshape(4, 8, 2, mesh.shape["lat"]), (*TM, "lat"))
    band = P(TM, "lat", None)
    in_specs = (
        P(TM, None, "lat", None),
        P(None, "lat", None),
        band,
        band,
        band,
        band,
        P(),
        P(),
        band,
        band,
    )
    out_specs = (P(TM, None, "lat", None), P(TM, None, "lat", None), band)
    return jax.shard_map(
        on_device, mesh=torus, in_specs=in_specs, out_specs=out_specs, check_vma=False
    )
```

```python
import jax
import jax.numpy as jnp
from jax import lax
from jax.experimental import pallas as pl
from jax.experimental.pallas import tpu as pltpu
from jax.sharding import Mesh
from jax.sharding import PartitionSpec as P

L = 5
TILE = 128
STEPS = 4
ROWS = 8
H = STEPS
W = ROWS + 2 * H
TM = ("tm_0", "tm_1", "tm_2")
FAR = ("tm_0", "tm_1")
NEAR = ("tm_2", "lat")
ROW = (8, TILE)


def lanes():
    return lax.broadcasted_iota(jnp.int32, ROW, 1)


class Shift:
    def __init__(self):
        lane = lanes()
        self.first = lane == 0
        self.last = lane == TILE - 1

    def east(self, v):
        r = pltpu.roll(v, TILE - 1, 1)
        return jnp.where(self.last, pltpu.roll(r, 7, 0), r)

    def west(self, v):
        r = pltpu.roll(v, 1, 1)
        return jnp.where(self.first, pltpu.roll(r, 1, 0), r)


def total(terms):
    while len(terms) > 1:
        terms = [a + b for a, b in zip(terms[::2], terms[1::2])] + (
            [terms[-1]] if len(terms) % 2 else []
        )
    return terms[0]


def centre(ce, cw, ky):
    return (1.0 - (ce + cw)) - 2.0 * ky


def forward(src, coef, c, rows, bufs, dst):
    sh = Shift()
    for step in range(STEPS):
        lo, hi = step + 1, rows - step - 1

        def get(r, step=step):
            if step == 0:
                return [src(l, r) for l in range(L)]
            return [bufs[(step - 1) % 2][l, r] for l in range(L)]

        above, here = get(lo - 1), get(lo)
        for r in range(lo, hi):
            below = get(r + 1)
            ce, cw, ky = coef(0, r), coef(1, r), coef(2, r)
            c0 = centre(ce, cw, ky)
            for l in range(L):
                v = here[l]
                terms = [
                    ce * sh.east(v),
                    cw * sh.west(v),
                    ky * (above[l] + below[l]),
                    c0 * v,
                ] + [c[L * l + m] * here[m] for m in range(L)]
                out = total(terms)
                if step == STEPS - 1:
                    dst(l, r, out)
                else:
                    bufs[step % 2][l, r] = out
            above, here = here, below


def adjoint(src, coef, c, rows, bufs, dst):
    sh = Shift()
    for step in range(STEPS):
        lo, hi = step + 1, rows - step - 1

        def get(r, step=step):
            if step == 0:
                v = [src(l, r) for l in range(L)]
            else:
                v = [bufs[(step - 1) % 2][l, r] for l in range(L)]
            ky = coef(2, r)
            return v, [ky * w for w in v]

        (_, above), (here, q) = get(lo - 1), get(lo)
        for r in range(lo, hi):
            after, below = get(r + 1)
            ce, cw, ky = coef(0, r), coef(1, r), coef(2, r)
            c0 = centre(ce, cw, ky)
            for l in range(L):
                w = here[l]
                terms = [
                    sh.west(ce * w),
                    sh.east(cw * w),
                    above[l] + below[l],
                    c0 * w,
                ] + [c[L * m + l] * here[m] for m in range(L)]
                out = total(terms)
                if step == STEPS - 1:
                    dst(l, r, out)
                else:
                    bufs[step % 2][l, r] = out
            above, here, q = q, after, below


def banded(up, own, down, first):
    def at(k, r):
        part = (up, own, down)[r // ROWS]
        return part[first + k, r % ROWS]

    return at


def place():
    j, n = 0, 1
    for axis in TM:
        j = j * lax.axis_size(axis) + lax.axis_index(axis)
        n = n * lax.axis_size(axis)
    return jnp.where(j == n - 1, 0.0, 1.0), jnp.where(j == 0, 1.0, 0.0)


def split(v):
    return jnp.swapaxes(jnp.stack([v[:, s * TILE : (s + 1) * TILE] for s in range(8)]), 0, 1)


def join_into(ref, index, rows):
    v = jnp.swapaxes(jnp.stack(rows), 0, 1)
    for s in range(8):
        ref[(*index, slice(None), slice(s * TILE, (s + 1) * TILE))] = v[s]


def pack_kernel(x_far, kx_far, ky_far, ux_far, out, x, k3, sems):
    copies = [
        pltpu.make_async_copy(x_far.at[0], x, sems.at[0]),
        pltpu.make_async_copy(kx_far, k3.at[pl.ds(0, 1)], sems.at[1]),
        pltpu.make_async_copy(ky_far, k3.at[pl.ds(1, 1)], sems.at[2]),
        pltpu.make_async_copy(ux_far, k3.at[pl.ds(2, 1)], sems.at[3]),
    ]
    for copy in copies:
        copy.start()
    for copy in copies[1:]:
        copy.wait()
    k, u = k3[0], 0.5 * k3[2]
    out[L] = split(k + u)
    out[L + 1] = split(k - u)
    out[L + 2] = split(k3[1])
    copies[0].wait()
    for l in range(L):
        out[l] = split(x[l])


def tiles(v):
    return jnp.swapaxes(jnp.stack([jnp.broadcast_to(v[:, s : s + 1], ROW) for s in range(8)]), 0, 1)


def aside_kernel(
    background, observed, coupling, var, obs_level, huber_class, bg, obs, c, keep, level, weight
):
    level[...] = tiles(obs_level[0].astype(jnp.float32))
    h = huber_class[0]
    weight[...] = tiles(jnp.where(h == 0, 1.0, 0.0) + jnp.where(h == 1, 0.5, 0.0) + jnp.where(h == 2, 0.25, 0.0))
    for l in range(L):
        bg[l] = split(background[l])
        keep[l] = jnp.broadcast_to(2.0 - 0.5 * var[:, l : l + 1], ROW)
        for m in range(L):
            c[L * l + m] = jnp.broadcast_to(coupling[l : l + 1, m : m + 1], ROW)
    obs[...] = split(observed[0])


def middle_kernel(up, own, down, out):
    for k in range(L):
        out[k, :H] = up[k, H:]
        out[k, H : H + ROWS] = own[k]
        out[k, H + ROWS :] = down[k, :H]


def forward_kernel(c, up, own, down, up_c, own_c, down_c, out, out_own, a, b):
    def dst(l, r, v):
        out[l, r - H] = v
        if ROWS <= r < 2 * ROWS:
            out_own[l, r - ROWS] = v

    forward(banded(up, own, down, 0), banded(up_c, own_c, down_c, L), c, 3 * ROWS, (a, b), dst)


def picked(level, values):
    out = jnp.where(level == 0, values[0], 0.0)
    for l in range(1, L):
        out = jnp.where(level == float(l), values[l], out)
    return out


def back_kernel(c, after, moved, up, own, down, obs, level, weight, ahead, o1, p, a, b):
    half = 0.5 * place()[0]
    for l in range(L):
        for r in range(W):
            ahead[l, r] = half * (after[l, r] - moved[l, r])
    for r in range(ROWS):
        o1[r] = 0.5 * weight[r] * (picked(level[r], [own[l, r] for l in range(L)]) - obs[r])
    coef = banded(up, own, down, L)

    def dst(l, r, v):
        r = r - H
        p[l, r] = jnp.where(level[r] == float(l), o1[r], 0.0) - v

    adjoint(lambda l, r: ahead[l, r], lambda k, r: coef(k, r + H), c, W, (a, b), dst)


def gradient_kernel(came, own, bg, p, d, g):
    first = place()[1]
    for l in range(L):
        for r in range(ROWS):
            v = 0.5 * (own[l, r] - (came[l, r] + first * bg[l, r]))
            d[l, r] = v
            g[l, r] = v + p[l, r]


def still_kernel(c, keep, d, ahead, up, own, down, level, o1, g0, a, b):
    coef = banded(up, own, down, L)

    def dst(l, r, v):
        r = r - H
        g0[l, r] = keep[l] * d[l, r] - v + jnp.where(level[r] == float(l), 1.5 * o1[r], 0.0)

    adjoint(lambda l, r: keep[l] * ahead[l, r], lambda k, r: coef(k, r + H), c, W, (a, b), dst)


def back_g_kernel(c, after, moved, up, own, down, g, level, weight, g0, hg, p, sums, ahead, a, b):
    some = place()[0]
    for l in range(L):
        for r in range(W):
            ahead[l, r] = some * (after[l, r] - moved[l, r])
    for r in range(ROWS):
        hg[r] = weight[r] * picked(level[r], [g[l, r] for l in range(L)])
    coef = banded(up, own, down, L)

    def dst(l, r, v):
        r = r - H
        p[l, r] = jnp.where(level[r] == float(l), hg[r], 0.0) - v

    adjoint(lambda l, r: ahead[l, r], lambda k, r: coef(k, r + H), c, W, (a, b), dst)
    for k, ref in enumerate((g, g0)):
        sums[k] = total([ref[l, r] * ref[l, r] for l in range(L) for r in range(ROWS)])


def sums_kernel(came, g, g0, p, early, u, g1, part):
    late = [[], []]
    for l in range(L):
        for r in range(ROWS):
            v = g[l, r] - came[l, r]
            u[l, r] = v
            one = -0.5 * (v + p[l, r])
            g1[l, r] = one
            late[0].append(g0[l, r] * one)
            late[1].append(one * one)
        late = [[total(terms)] for terms in late]
    lane = lax.broadcasted_iota(jnp.int32, (1, TILE), 1)
    row = jnp.zeros((1, TILE), jnp.float32)
    for k, v in enumerate((early[0], early[1], late[0][0], late[1][0])):
        s = jnp.sum(jnp.sum(v, axis=0, keepdims=True), axis=1, keepdims=True)
        row = jnp.where(lane == k, s, row)
    for i in range(part.shape[0]):
        part[i] = row


def again_kernel(parts, out):
    s = total([parts[i] for i in range(parts.shape[0])])
    for i in range(out.shape[0]):
        out[i] = s


def last_kernel(
    count, parts, keep, own, g, g0, g1, d, u, o1, hg, state_far, multipliers_far, obs_far, state, multipliers, obs, sems
):
    row = total([parts[i] for i in range(parts.shape[0])])
    lane = lax.broadcasted_iota(jnp.int32, (1, TILE), 1)
    sg, s00, s01, s11 = [
        jnp.broadcast_to(jnp.sum(jnp.where(lane == k, row, 0.0), axis=1, keepdims=True), ROW) / count
        for k in range(4)
    ]
    first = 0.3 / jnp.sqrt(sg + 1e-06)
    mean = jnp.maximum(s00 + first * (2.0 * s01 + first * s11), 0.0)
    second = 0.3 / jnp.sqrt(mean + 1e-06)
    half = 0.5 * first
    copies = []

    def send(here, far):
        copies.append(pltpu.make_async_copy(here, far, sems.at[len(copies)]))
        copies[-1].start()

    join_into(obs, (0,), [1.5 * o1[r] - half * hg[r] for r in range(ROWS)])
    send(obs, obs_far)
    for l in range(L):
        join_into(multipliers, (l,), [keep[l] * d[l, r] - half * u[l, r] for r in range(ROWS)])
        send(multipliers.at[l], multipliers_far.at[0, l])
        join_into(
            state,
            (l,),
            [
                own[l, r] - first * g[l, r] - second * (g0[l, r] + first * g1[l, r])
                for r in range(ROWS)
            ],
        )
        send(state.at[l], state_far.at[0, l])
    for copy in copies:
        copy.wait()


VM = pl.BlockSpec(memory_space=pltpu.VMEM)
FARM = pl.BlockSpec(memory_space=pltpu.HBM)


def call(kernel, outs, scratch=(), us=1.0, far_in=False, far_out=False):
    def run(*args):
        if far_in:
            args = [pltpu.with_memory_space_constraint(a, pltpu.HBM) for a in args]
        return pl.pallas_call(
            kernel,
            out_shape=[jax.ShapeDtypeStruct(s, jnp.float32) for s in outs],
            in_specs=[FARM if far_in else VM] * len(args),
            out_specs=[FARM if far_out else VM] * len(outs),
            scratch_shapes=[pltpu.VMEM(s, jnp.float32) if isinstance(s, tuple) else s for s in scratch],
            compiler_params=pltpu.CompilerParams(vmem_limit_bytes=16 * 2**20),
            cost_estimate=pl.CostEstimate(
                flops=int(us * 4e6), bytes_accessed=sum(4 * a.size for a in args), transcendentals=0
            ),
        )(*args)

    return run


def rows_of(k, n):
    return (k, n, *ROW)


def shifted(x, axis, by):
    count = lax.axis_size(axis)
    return lax.ppermute(x, axis, [(i, i + by) for i in range(count) if 0 <= i + by < count])


def exchanged(x, axis):
    return lax.all_to_all(x, axis, 0, 0, tiled=True)


def on_device(
    x_init, background, observed, diff_lon, diff_lat, drift, coupling, model_var, obs_level, huber_class
):
    band, wide = rows_of(L, ROWS), rows_of(L, W)
    whole = (L, ROWS, 8 * TILE)
    cells = (ROWS, *ROW)
    two, two_w = [rows_of(L, 3 * ROWS)] * 2, [wide] * 2
    count = float(L * ROWS * 8 * TILE * lax.axis_size(TM) * lax.axis_size("lat"))
    (own,) = call(
        pack_kernel,
        [rows_of(L + 3, ROWS)],
        [whole, (3, *whole[1:]), pltpu.SemaphoreType.DMA((4,))],
        far_in=True,
    )(x_init, diff_lon, diff_lat, drift)
    up, down = shifted(own, "lat", 1), shifted(own, "lat", -1)
    bg, obs, c, keep, level, weight = call(
        aside_kernel, [band, cells, (L * L, *ROW), (L, *ROW), cells, cells]
    )(background, observed, coupling, model_var[None], obs_level, huber_class)
    up, down, bg, obs, c, keep, level, weight = lax.optimization_barrier(
        (up, down, bg, obs, c, keep, level, weight)
    )

    (wide_x,) = call(middle_kernel, [wide])(up, own, down)
    after = shifted(wide_x, TM, -1)
    moved, moved_own = call(forward_kernel, [wide, band], two, 2.0)(c, up, own, down, up, own, down)
    came = shifted(moved_own, TM, 1)
    ahead, o1, p = call(back_kernel, [wide, cells, band], two_w, 1.5)(
        c, after, moved, up, own, down, obs, level, weight
    )
    d, g = call(gradient_kernel, [band, band], us=0.2)(came, own, bg, p)

    up_g, down_g = shifted(g, "lat", 1), shifted(g, "lat", -1)
    (g0,) = call(still_kernel, [band], two_w, 1.5)(c, keep, d, ahead, up, own, down, level, o1)
    up_g, down_g, g0 = lax.optimization_barrier((up_g, down_g, g0))
    (wide_g,) = call(middle_kernel, [wide])(up_g, g, down_g)
    after_g = shifted(wide_g, TM, -1)
    moved_g, moved_g_own = call(forward_kernel, [wide, band], two, 2.0)(
        c, up_g, g, down_g, up, own, down
    )
    came_g = shifted(moved_g_own, TM, 1)
    hg, q, early = call(back_g_kernel, [cells, band, (2, *ROW)], [wide] + two_w, 1.5)(
        c, after_g, moved_g, up, own, down, g, level, weight, g0
    )
    u, g1, part = call(sums_kernel, [band, band, (lax.axis_size(NEAR), 1, TILE)], us=0.3)(
        came_g, g, g0, q, early
    )
    (part,) = call(again_kernel, [(lax.axis_size(FAR), 1, TILE)], us=0.1)(exchanged(part, NEAR))
    part = exchanged(part, FAR)

    def finish(*refs):
        last_kernel(count, *refs)

    outs = call(
        finish,
        [(1, *whole), (1, *whole), (1, *whole[1:])],
        [whole, whole, (1, *whole[1:]), pltpu.SemaphoreType.DMA((2 * L + 1,))],
        far_out=True,
    )(part, keep, own, g, g0, g1, d, u, o1, hg)
    return tuple(outs)


def solution(mesh):
    torus = Mesh(mesh.devices.reshape(4, 8, 2, mesh.shape["lat"]), (*TM, "lat"))
    band = P(TM, "lat", None)
    in_specs = (
        P(TM, None, "lat", None),
        P(None, "lat", None),
        band,
        band,
        band,
        band,
        P(),
        P(),
        band,
        band,
    )
    out_specs = (P(TM, None, "lat", None), P(TM, None, "lat", None), band)
    return jax.shard_map(
        on_device, mesh=torus, in_specs=in_specs, out_specs=out_specs, check_vma=False
    )
```

```python
import jax
import jax.numpy as jnp
from jax import lax
from jax.experimental import pallas as pl
from jax.experimental.pallas import tpu as pltpu
from jax.sharding import Mesh
from jax.sharding import PartitionSpec as P

L = 5
TILE = 128
STEPS = 4
ROWS = 8
H = STEPS
W = ROWS + 2 * H
TM = ("tm_0", "tm_1", "tm_2")
FAR = ("tm_0", "tm_1")
NEAR = ("tm_2", "lat")
ROW = (8, TILE)


def lanes():
    return lax.broadcasted_iota(jnp.int32, ROW, 1)


class Shift:
    def __init__(self):
        lane = lanes()
        self.first = lane == 0
        self.last = lane == TILE - 1

    def east(self, v):
        r = pltpu.roll(v, TILE - 1, 1)
        return jnp.where(self.last, pltpu.roll(r, 7, 0), r)

    def west(self, v):
        r = pltpu.roll(v, 1, 1)
        return jnp.where(self.first, pltpu.roll(r, 1, 0), r)


def total(terms):
    while len(terms) > 1:
        terms = [a + b for a, b in zip(terms[::2], terms[1::2])] + (
            [terms[-1]] if len(terms) % 2 else []
        )
    return terms[0]


def centre(ce, cw, ky):
    return (1.0 - (ce + cw)) - 2.0 * ky


def forward(src, coef, c, rows, bufs, dst):
    sh = Shift()
    for step in range(STEPS):
        lo, hi = step + 1, rows - step - 1

        def get(r, step=step):
            if step == 0:
                return [src(l, r) for l in range(L)]
            return [bufs[(step - 1) % 2][l, r] for l in range(L)]

        above, here = get(lo - 1), get(lo)
        for r in range(lo, hi):
            below = get(r + 1)
            ce, cw, ky = coef(0, r), coef(1, r), coef(2, r)
            c0 = centre(ce, cw, ky)
            for l in range(L):
                v = here[l]
                terms = [
                    ce * sh.east(v),
                    cw * sh.west(v),
                    ky * (above[l] + below[l]),
                    c0 * v,
                ] + [c[L * l + m] * here[m] for m in range(L)]
                out = total(terms)
                if step == STEPS - 1:
                    dst(l, r, out)
                else:
                    bufs[step % 2][l, r] = out
            above, here = here, below


def adjoint(src, coef, c, rows, bufs, dst):
    sh = Shift()
    for step in range(STEPS):
        lo, hi = step + 1, rows - step - 1

        def get(r, step=step):
            if step == 0:
                v = [src(l, r) for l in range(L)]
            else:
                v = [bufs[(step - 1) % 2][l, r] for l in range(L)]
            ky = coef(2, r)
            return v, [ky * w for w in v]

        (_, above), (here, q) = get(lo - 1), get(lo)
        for r in range(lo, hi):
            after, below = get(r + 1)
            ce, cw, ky = coef(0, r), coef(1, r), coef(2, r)
            c0 = centre(ce, cw, ky)
            for l in range(L):
                w = here[l]
                terms = [
                    sh.west(ce * w),
                    sh.east(cw * w),
                    above[l] + below[l],
                    c0 * w,
                ] + [c[L * m + l] * here[m] for m in range(L)]
                out = total(terms)
                if step == STEPS - 1:
                    dst(l, r, out)
                else:
                    bufs[step % 2][l, r] = out
            above, here, q = q, after, below


def banded(up, own, down, first):
    def at(k, r):
        part = (up, own, down)[r // ROWS]
        return part[first + k, r % ROWS]

    return at


def place():
    j, n = 0, 1
    for axis in TM:
        j = j * lax.axis_size(axis) + lax.axis_index(axis)
        n = n * lax.axis_size(axis)
    return jnp.where(j == n - 1, 0.0, 1.0), jnp.where(j == 0, 1.0, 0.0)


def split(v):
    return jnp.swapaxes(jnp.stack([v[:, s * TILE : (s + 1) * TILE] for s in range(8)]), 0, 1)


def join_into(ref, index, rows):
    v = jnp.swapaxes(jnp.stack(rows), 0, 1)
    for s in range(8):
        ref[(*index, slice(None), slice(s * TILE, (s + 1) * TILE))] = v[s]


def pack_kernel(x_far, kx_far, ky_far, ux_far, out, x, k3, sems):
    copies = [
        pltpu.make_async_copy(x_far.at[0], x, sems.at[0]),
        pltpu.make_async_copy(kx_far, k3.at[pl.ds(0, 1)], sems.at[1]),
        pltpu.make_async_copy(ky_far, k3.at[pl.ds(1, 1)], sems.at[2]),
        pltpu.make_async_copy(ux_far, k3.at[pl.ds(2, 1)], sems.at[3]),
    ]
    for copy in copies:
        copy.start()
    for copy in copies[1:]:
        copy.wait()
    k, u = k3[0], 0.5 * k3[2]
    out[L] = split(k + u)
    out[L + 1] = split(k - u)
    out[L + 2] = split(k3[1])
    copies[0].wait()
    for l in range(L):
        out[l] = split(x[l])


def tiles(v):
    return jnp.swapaxes(jnp.stack([jnp.broadcast_to(v[:, s : s + 1], ROW) for s in range(8)]), 0, 1)


def aside_kernel(
    own, background, observed, coupling, var, obs_level, huber_class, x, bg, obs, c, keep, level, weight
):
    x[...] = own[:L]
    level[...] = tiles(obs_level[0].astype(jnp.float32))
    h = huber_class[0]
    weight[...] = tiles(jnp.where(h == 0, 1.0, 0.0) + jnp.where(h == 1, 0.5, 0.0) + jnp.where(h == 2, 0.25, 0.0))
    for l in range(L):
        bg[l] = split(background[l])
        keep[l] = jnp.broadcast_to(2.0 - 0.5 * var[:, l : l + 1], ROW)
        for m in range(L):
            c[L * l + m] = jnp.broadcast_to(coupling[l : l + 1, m : m + 1], ROW)
    obs[...] = split(observed[0])


def odd(axis):
    return lax.rem(lax.axis_index(axis), 2) == 1


def forward_kernel(c, first, second, own, up, down, moved, one, two, a, b):
    upper = odd("lat")
    for k in range(L + 3):
        for r in range(ROWS):
            up[k, r] = jnp.where(upper, second[k, r], first[k, r])
            down[k, r] = jnp.where(upper, first[k, r], second[k, r])
    send(c, up, own, down, up, own, down, moved, one, two, a, b)


def forward_g_kernel(c, first, second, own, up_c, own_c, down_c, moved, one, two, up, down, a, b):
    upper = odd("lat")
    for k in range(L):
        for r in range(ROWS):
            up[k, r] = jnp.where(upper, second[k, r], first[k, r])
            down[k, r] = jnp.where(upper, first[k, r], second[k, r])
    send(c, up, own, down, up_c, own_c, down_c, moved, one, two, a, b)


def send(c, up, own, down, up_c, own_c, down_c, moved, one, two, a, b):
    ahead = odd(TM[-1])

    def dst(l, r, v):
        moved[l, r - H] = v
        if ROWS <= r < 2 * ROWS:
            r = r - ROWS
            halo = up[l, H + r] if r < H else down[l, r - H]
            one[l, r] = jnp.where(ahead, v, halo)
            two[l, r] = jnp.where(ahead, halo, v)

    forward(banded(up, own, down, 0), banded(up_c, own_c, down_c, L), c, 3 * ROWS, (a, b), dst)


def receive(one, two, after, moved, factor, out):
    ahead = odd(TM[-1])
    for l in range(L):
        for r in range(W):
            if H <= r < H + ROWS:
                v = after[l, r - H]
            else:
                at = r if r < H else r - ROWS
                v = jnp.where(ahead, one[l, at], two[l, at])
            out[l, r] = factor * (v - moved[l, r])
    return lambda l, r: jnp.where(ahead, two[l, r], one[l, r])


def picked(level, values):
    out = jnp.where(level == 0, values[0], 0.0)
    for l in range(1, L):
        out = jnp.where(level == float(l), values[l], out)
    return out


def back_kernel(
    c, one, two, after, moved, up, own, down, bg, obs, level, weight, ahead, o1, d, g, a, b
):
    some, first = place()
    came = receive(one, two, after, moved, 0.5 * some, ahead)
    for r in range(ROWS):
        o1[r] = 0.5 * weight[r] * (picked(level[r], [own[l, r] for l in range(L)]) - obs[r])
    coef = banded(up, own, down, L)

    def dst(l, r, v):
        r = r - H
        one = 0.5 * (own[l, r] - (came(l, r) + first * bg[l, r]))
        d[l, r] = one
        g[l, r] = one - v + jnp.where(level[r] == float(l), o1[r], 0.0)

    adjoint(lambda l, r: ahead[l, r], lambda k, r: coef(k, r + H), c, W, (a, b), dst)


def still_kernel(c, keep, d, ahead, up, own, down, level, o1, g, g0, g_out, a, b):
    g_out[...] = g[...]
    coef = banded(up, own, down, L)

    def dst(l, r, v):
        r = r - H
        g0[l, r] = keep[l] * d[l, r] - v + jnp.where(level[r] == float(l), 1.5 * o1[r], 0.0)

    adjoint(lambda l, r: keep[l] * ahead[l, r], lambda k, r: coef(k, r + H), c, W, (a, b), dst)


def back_g_kernel(
    c, one, two, after, moved, up, own, down, g, level, weight, g0, u, g1, hg, part, ahead, a, b
):
    came = receive(one, two, after, moved, place()[0], ahead)
    for r in range(ROWS):
        hg[r] = weight[r] * picked(level[r], [g[l, r] for l in range(L)])
    coef = banded(up, own, down, L)
    sums = [[], [], [], []]

    def dst(l, r, v):
        r = r - H
        now = g[l, r] - came(l, r)
        u[l, r] = now
        one = -0.5 * (now - v + jnp.where(level[r] == float(l), hg[r], 0.0))
        g1[l, r] = one
        for k, term in enumerate((g[l, r] * g[l, r], g0[l, r] * g0[l, r], g0[l, r] * one, one * one)):
            sums[k].append(term)
            if len(sums[k]) == L:
                sums[k] = [total(sums[k])]

    adjoint(lambda l, r: ahead[l, r], lambda k, r: coef(k, r + H), c, W, (a, b), dst)
    lane = lax.broadcasted_iota(jnp.int32, (1, TILE), 1)
    row = jnp.zeros((1, TILE), jnp.float32)
    for k in range(4):
        s = jnp.sum(jnp.sum(total(sums[k]), axis=0, keepdims=True), axis=1, keepdims=True)
        row = jnp.where(lane == k, s, row)
    for i in range(part.shape[0]):
        part[i] = row


def again_kernel(parts, out):
    s = total([parts[i] for i in range(parts.shape[0])])
    for i in range(out.shape[0]):
        out[i] = s


def last_kernel(
    count, parts, keep, own, g, g0, g1, d, u, o1, hg, state_far, multipliers_far, obs_far, state, multipliers, obs, sems
):
    row = total([parts[i] for i in range(parts.shape[0])])
    lane = lax.broadcasted_iota(jnp.int32, (1, TILE), 1)
    sg, s00, s01, s11 = [
        jnp.broadcast_to(jnp.sum(jnp.where(lane == k, row, 0.0), axis=1, keepdims=True), ROW) / count
        for k in range(4)
    ]
    first = 0.3 / jnp.sqrt(sg + 1e-06)
    mean = jnp.maximum(s00 + first * (2.0 * s01 + first * s11), 0.0)
    second = 0.3 / jnp.sqrt(mean + 1e-06)
    half = 0.5 * first
    copies = []

    def send(here, far):
        copies.append(pltpu.make_async_copy(here, far, sems.at[len(copies)]))
        copies[-1].start()

    join_into(obs, (0,), [1.5 * o1[r] - half * hg[r] for r in range(ROWS)])
    send(obs, obs_far)
    for l in range(L):
        join_into(multipliers, (l,), [keep[l] * d[l, r] - half * u[l, r] for r in range(ROWS)])
        send(multipliers.at[l], multipliers_far.at[0, l])
        join_into(
            state,
            (l,),
            [
                own[l, r] - first * g[l, r] - second * (g0[l, r] + first * g1[l, r])
                for r in range(ROWS)
            ],
        )
        send(state.at[l], state_far.at[0, l])
    for copy in copies:
        copy.wait()


VM = pl.BlockSpec(memory_space=pltpu.VMEM)
FARM = pl.BlockSpec(memory_space=pltpu.HBM)


def call(kernel, outs, scratch=(), us=1.0, far_in=False, far_out=False):
    def run(*args):
        if far_in:
            args = [pltpu.with_memory_space_constraint(a, pltpu.HBM) for a in args]
        return pl.pallas_call(
            kernel,
            out_shape=[jax.ShapeDtypeStruct(s, jnp.float32) for s in outs],
            in_specs=[FARM if far_in else VM] * len(args),
            out_specs=[FARM if far_out else VM] * len(outs),
            scratch_shapes=[pltpu.VMEM(s, jnp.float32) if isinstance(s, tuple) else s for s in scratch],
            compiler_params=pltpu.CompilerParams(vmem_limit_bytes=16 * 2**20),
            cost_estimate=pl.CostEstimate(
                flops=int(us * 4e6), bytes_accessed=sum(4 * a.size for a in args), transcendentals=0
            ),
        )(*args)

    return run


def rows_of(k, n):
    return (k, n, *ROW)


def shifted(x, axis, by):
    count = lax.axis_size(axis)
    return lax.ppermute(x, axis, [(i, i + by) for i in range(count) if 0 <= i + by < count])


def swapped(*args):
    *arrays, axis = args
    count = lax.axis_size(axis)
    out = []
    for x, start in zip((arrays[0], arrays[-1]), (1, 0)):
        lows = range(start, count - 1, 2)
        out.append(lax.ppermute(x, axis, [p for i in lows for p in ((i, i + 1), (i + 1, i))]))
    return out


def exchanged(x, axis):
    return lax.all_to_all(x, axis, 0, 0, tiled=True)


def on_device(
    x_init, background, observed, diff_lon, diff_lat, drift, coupling, model_var, obs_level, huber_class
):
    band, wide = rows_of(L, ROWS), rows_of(L, W)
    whole = (L, ROWS, 8 * TILE)
    cells = (ROWS, *ROW)
    two, two_w = [rows_of(L, 3 * ROWS)] * 2, [wide] * 2
    count = float(L * ROWS * 8 * TILE * lax.axis_size(TM) * lax.axis_size("lat"))
    (own,) = call(
        pack_kernel,
        [rows_of(L + 3, ROWS)],
        [whole, (3, *whole[1:]), pltpu.SemaphoreType.DMA((4,))],
        far_in=True,
    )(x_init, diff_lon, diff_lat, drift)
    first, second = swapped(own, "lat")
    x, bg, obs, c, keep, level, weight = call(
        aside_kernel, [band, band, cells, (L * L, *ROW), (L, *ROW), cells, cells]
    )(own, background, observed, coupling, model_var[None], obs_level, huber_class)
    after = shifted(x, TM, -1)
    first, second, bg, obs, c, keep, level, weight = lax.optimization_barrier(
        (first, second, bg, obs, c, keep, level, weight)
    )

    three = rows_of(L + 3, ROWS)
    up, down, moved, *sent = call(forward_kernel, [three, three, wide, band, band], two, 2.0)(
        c, first, second, own
    )
    ahead, o1, d, g = call(back_kernel, [wide, cells, band, band], two_w, 1.5)(
        c, *swapped(*sent, TM), after, moved, up, own, down, bg, obs, level, weight
    )

    first, second = swapped(g, "lat")
    g0, g_copy = call(still_kernel, [band, band], two_w, 1.5)(
        c, keep, d, ahead, up, own, down, level, o1, g
    )
    after_g = shifted(g_copy, TM, -1)
    first, second, g0 = lax.optimization_barrier((first, second, g0))
    moved_g, *sent = call(forward_g_kernel, [wide, band, band], [band, band] + two, 2.0)(
        c, first, second, g, up, own, down
    )
    u, g1, hg, part = call(
        back_g_kernel,
        [band, band, cells, (lax.axis_size(NEAR), 1, TILE)],
        [wide] + two_w,
        1.5,
    )(c, *swapped(*sent, TM), after_g, moved_g, up, own, down, g, level, weight, g0)
    (part,) = call(again_kernel, [(lax.axis_size(FAR), 1, TILE)], us=0.1)(exchanged(part, NEAR))
    part = exchanged(part, FAR)

    def finish(*refs):
        last_kernel(count, *refs)

    outs = call(
        finish,
        [(1, *whole), (1, *whole), (1, *whole[1:])],
        [whole, whole, (1, *whole[1:]), pltpu.SemaphoreType.DMA((2 * L + 1,))],
        far_out=True,
    )(part, keep, own, g, g0, g1, d, u, o1, hg)
    return tuple(outs)


def solution(mesh):
    torus = Mesh(mesh.devices.reshape(4, 8, 2, mesh.shape["lat"]), (*TM, "lat"))
    band = P(TM, "lat", None)
    in_specs = (
        P(TM, None, "lat", None),
        P(None, "lat", None),
        band,
        band,
        band,
        band,
        P(),
        P(),
        band,
        band,
    )
    out_specs = (P(TM, None, "lat", None), P(TM, None, "lat", None), band)
    return jax.shard_map(
        on_device, mesh=torus, in_specs=in_specs, out_specs=out_specs, check_vma=False
    )
```

```python
import jax
import jax.numpy as jnp
from jax import lax
from jax.experimental import pallas as pl
from jax.experimental.pallas import tpu as pltpu
from jax.sharding import Mesh
from jax.sharding import PartitionSpec as P

L = 5
TILE = 128
STEPS = 4
ROWS = 8
H = STEPS
W = ROWS + 2 * H
TM = ("tm_0", "tm_1", "tm_2")
FAR = ("tm_0", "tm_1")
NEAR = ("tm_2", "lat")
ROW = (8, TILE)


def lanes():
    return lax.broadcasted_iota(jnp.int32, ROW, 1)


class Shift:
    def __init__(self):
        lane = lanes()
        self.first = lane == 0
        self.last = lane == TILE - 1

    def east(self, v):
        r = pltpu.roll(v, TILE - 1, 1)
        return jnp.where(self.last, pltpu.roll(r, 7, 0), r)

    def west(self, v):
        r = pltpu.roll(v, 1, 1)
        return jnp.where(self.first, pltpu.roll(r, 1, 0), r)


def total(terms):
    while len(terms) > 1:
        terms = [a + b for a, b in zip(terms[::2], terms[1::2])] + (
            [terms[-1]] if len(terms) % 2 else []
        )
    return terms[0]


def centre(ce, cw, ky):
    return (1.0 - (ce + cw)) - 2.0 * ky


def forward(src, coef, c, rows, bufs, dst):
    sh = Shift()
    for step in range(STEPS):
        lo, hi = step + 1, rows - step - 1

        def get(r, step=step):
            if step == 0:
                return [src(l, r) for l in range(L)]
            return [bufs[(step - 1) % 2][l, r] for l in range(L)]

        above, here = get(lo - 1), get(lo)
        for r in range(lo, hi):
            below = get(r + 1)
            ce, cw, ky = coef(0, r), coef(1, r), coef(2, r)
            c0 = centre(ce, cw, ky)
            for l in range(L):
                v = here[l]
                terms = [
                    ce * sh.east(v),
                    cw * sh.west(v),
                    ky * (above[l] + below[l]),
                    c0 * v,
                ] + [c[L * l + m] * here[m] for m in range(L)]
                out = total(terms)
                if step == STEPS - 1:
                    dst(l, r, out)
                else:
                    bufs[step % 2][l, r] = out
            above, here = here, below


def adjoint(src, coef, c, rows, bufs, dst):
    sh = Shift()
    for step in range(STEPS):
        lo, hi = step + 1, rows - step - 1

        def get(r, step=step):
            if step == 0:
                v = [src(l, r) for l in range(L)]
            else:
                v = [bufs[(step - 1) % 2][l, r] for l in range(L)]
            ky = coef(2, r)
            return v, [ky * w for w in v]

        (_, above), (here, q) = get(lo - 1), get(lo)
        for r in range(lo, hi):
            after, below = get(r + 1)
            ce, cw, ky = coef(0, r), coef(1, r), coef(2, r)
            c0 = centre(ce, cw, ky)
            for l in range(L):
                w = here[l]
                terms = [
                    sh.west(ce * w),
                    sh.east(cw * w),
                    above[l] + below[l],
                    c0 * w,
                ] + [c[L * m + l] * here[m] for m in range(L)]
                out = total(terms)
                if step == STEPS - 1:
                    dst(l, r, out)
                else:
                    bufs[step % 2][l, r] = out
            above, here, q = q, after, below


def banded(up, own, down, first):
    def at(k, r):
        part = (up, own, down)[r // ROWS]
        return part[first + k, r % ROWS]

    return at


def place():
    j, n = 0, 1
    for axis in TM:
        j = j * lax.axis_size(axis) + lax.axis_index(axis)
        n = n * lax.axis_size(axis)
    return jnp.where(j == n - 1, 0.0, 1.0), jnp.where(j == 0, 1.0, 0.0)


def split(v):
    return jnp.swapaxes(jnp.stack([v[:, s * TILE : (s + 1) * TILE] for s in range(8)]), 0, 1)


def join_into(ref, index, rows):
    v = jnp.swapaxes(jnp.stack(rows), 0, 1)
    for s in range(8):
        ref[(*index, slice(None), slice(s * TILE, (s + 1) * TILE))] = v[s]


def pack_kernel(x_far, kx_far, ky_far, ux_far, out, x, k3, sems):
    copies = [
        pltpu.make_async_copy(x_far.at[0], x, sems.at[0]),
        pltpu.make_async_copy(kx_far, k3.at[pl.ds(0, 1)], sems.at[1]),
        pltpu.make_async_copy(ky_far, k3.at[pl.ds(1, 1)], sems.at[2]),
        pltpu.make_async_copy(ux_far, k3.at[pl.ds(2, 1)], sems.at[3]),
    ]
    for copy in copies:
        copy.start()
    for copy in copies[1:]:
        copy.wait()
    k, u = k3[0], 0.5 * k3[2]
    out[L] = split(k + u)
    out[L + 1] = split(k - u)
    out[L + 2] = split(k3[1])
    copies[0].wait()
    for l in range(L):
        out[l] = split(x[l])


def tiles(v):
    return jnp.swapaxes(jnp.stack([jnp.broadcast_to(v[:, s : s + 1], ROW) for s in range(8)]), 0, 1)


def aside_kernel(
    own, background, observed, coupling, var, obs_level, huber_class, x, bg, obs, c, keep, level, weight
):
    x[...] = own[:L]
    level[...] = tiles(obs_level[0].astype(jnp.float32))
    h = huber_class[0]
    weight[...] = tiles(jnp.where(h == 0, 1.0, 0.0) + jnp.where(h == 1, 0.5, 0.0) + jnp.where(h == 2, 0.25, 0.0))
    for l in range(L):
        bg[l] = split(background[l])
        keep[l] = jnp.broadcast_to(2.0 - 0.5 * var[:, l : l + 1], ROW)
        for m in range(L):
            c[L * l + m] = jnp.broadcast_to(coupling[l : l + 1, m : m + 1], ROW)
    obs[...] = split(observed[0])


def odd(axis):
    return lax.rem(lax.axis_index(axis), 2) == 1


def sides(first, second, fields, up, down):
    below = lax.rem(lax.axis_index("lat") + lax.axis_index(TM[-1]), 2) == 1
    for k in range(fields):
        for r in range(ROWS):
            up[k, r] = jnp.where(below, second[k, r], first[k, r])
            down[k, r] = jnp.where(below, first[k, r], second[k, r])


def forward_kernel(c, first, second, own, up, down, moved, one, two, a, b):
    sides(first, second, L + 3, up, down)
    send(c, up, own, down, up, own, down, moved, one, two, a, b)


def forward_g_kernel(c, first, second, own, up_c, own_c, down_c, up, down, moved, one, two, a, b):
    sides(first, second, L, up, down)
    send(c, up, own, down, up_c, own_c, down_c, moved, one, two, a, b)


def send(c, up, own, down, up_c, own_c, down_c, moved, one, two, a, b):
    ahead = odd(TM[-1])
    field, coef = banded(up, own, down, 0), banded(up_c, own_c, down_c, L)

    def dst(l, r, v):
        r = r - H
        moved[l, r] = v
        halo = up[l, H + r] if r < H else down[l, r - H]
        one[l, r] = jnp.where(ahead, v, halo)
        two[l, r] = jnp.where(ahead, halo, v)

    forward(lambda l, r: field(l, r + H), lambda k, r: coef(k, r + H), c, W, (a, b), dst)


def halo_kernel(c, up, own, down, up_c, own_c, down_c, moved, a, b):
    field, coef = banded(up, own, down, 0), banded(up_c, own_c, down_c, L)
    for first, to in ((0, 0), (ROWS + H, H)):

        def dst(l, r, v, to=to):
            moved[l, to + r - H] = v

        forward(
            lambda l, r, first=first: field(l, first + r),
            lambda k, r, first=first: coef(k, first + r),
            c,
            3 * H,
            (a, b),
            dst,
        )


def receive(one, two, after, moved, moved_halo, factor, out):
    ahead = odd(TM[-1])
    for l in range(L):
        for r in range(W):
            if H <= r < H + ROWS:
                v = after[l, r - H] - moved[l, r - H]
            else:
                at = r if r < H else r - ROWS
                v = jnp.where(ahead, one[l, at], two[l, at]) - moved_halo[l, at]
            out[l, r] = factor * v
    return lambda l, r: jnp.where(ahead, two[l, r], one[l, r])


def picked(level, values):
    out = jnp.where(level == 0, values[0], 0.0)
    for l in range(1, L):
        out = jnp.where(level == float(l), values[l], out)
    return out


def back_kernel(
    c, one, two, after, moved, moved_halo, up, own, down, bg, obs, level, weight, ahead, o1, d, g, a, b
):
    some, first = place()
    came = receive(one, two, after, moved, moved_halo, 0.5 * some, ahead)
    for r in range(ROWS):
        o1[r] = 0.5 * weight[r] * (picked(level[r], [own[l, r] for l in range(L)]) - obs[r])
    coef = banded(up, own, down, L)

    def dst(l, r, v):
        r = r - H
        one = 0.5 * (own[l, r] - (came(l, r) + first * bg[l, r]))
        d[l, r] = one
        g[l, r] = one - v + jnp.where(level[r] == float(l), o1[r], 0.0)

    adjoint(lambda l, r: ahead[l, r], lambda k, r: coef(k, r + H), c, W, (a, b), dst)


def still_kernel(c, keep, d, ahead, up, own, down, level, o1, g, g0, g_out, a, b):
    g_out[...] = g[...]
    coef = banded(up, own, down, L)

    def dst(l, r, v):
        r = r - H
        g0[l, r] = keep[l] * d[l, r] - v + jnp.where(level[r] == float(l), 1.5 * o1[r], 0.0)

    adjoint(lambda l, r: keep[l] * ahead[l, r], lambda k, r: coef(k, r + H), c, W, (a, b), dst)


def back_g_kernel(
    c, one, two, after, moved, moved_halo, up, own, down, g, level, weight, g0, u, g1, hg, part, ahead, a, b
):
    came = receive(one, two, after, moved, moved_halo, place()[0], ahead)
    for r in range(ROWS):
        hg[r] = weight[r] * picked(level[r], [g[l, r] for l in range(L)])
    coef = banded(up, own, down, L)
    sums = [[], [], [], []]

    def dst(l, r, v):
        r = r - H
        now = g[l, r] - came(l, r)
        u[l, r] = now
        one = -0.5 * (now - v + jnp.where(level[r] == float(l), hg[r], 0.0))
        g1[l, r] = one
        for k, term in enumerate((g[l, r] * g[l, r], g0[l, r] * g0[l, r], g0[l, r] * one, one * one)):
            sums[k].append(term)
            if len(sums[k]) == L:
                sums[k] = [total(sums[k])]

    adjoint(lambda l, r: ahead[l, r], lambda k, r: coef(k, r + H), c, W, (a, b), dst)
    lane = lax.broadcasted_iota(jnp.int32, (1, TILE), 1)
    row = jnp.zeros((1, TILE), jnp.float32)
    for k in range(4):
        s = jnp.sum(jnp.sum(total(sums[k]), axis=0, keepdims=True), axis=1, keepdims=True)
        row = jnp.where(lane == k, s, row)
    for i in range(part.shape[0]):
        part[i] = row


def again_kernel(parts, out):
    s = total([parts[i] for i in range(parts.shape[0])])
    for i in range(out.shape[0]):
        out[i] = s


def last_kernel(
    count, parts, keep, own, g, g0, g1, d, u, o1, hg, state_far, multipliers_far, obs_far, state, multipliers, obs, sems
):
    row = total([parts[i] for i in range(parts.shape[0])])
    lane = lax.broadcasted_iota(jnp.int32, (1, TILE), 1)
    sg, s00, s01, s11 = [
        jnp.broadcast_to(jnp.sum(jnp.where(lane == k, row, 0.0), axis=1, keepdims=True), ROW) / count
        for k in range(4)
    ]
    first = 0.3 / jnp.sqrt(sg + 1e-06)
    mean = jnp.maximum(s00 + first * (2.0 * s01 + first * s11), 0.0)
    second = 0.3 / jnp.sqrt(mean + 1e-06)
    half = 0.5 * first
    copies = []

    def send(here, far):
        copies.append(pltpu.make_async_copy(here, far, sems.at[len(copies)]))
        copies[-1].start()

    join_into(obs, (0,), [1.5 * o1[r] - half * hg[r] for r in range(ROWS)])
    send(obs, obs_far)
    for l in range(L):
        join_into(multipliers, (l,), [keep[l] * d[l, r] - half * u[l, r] for r in range(ROWS)])
        send(multipliers.at[l], multipliers_far.at[0, l])
        join_into(
            state,
            (l,),
            [
                own[l, r] - first * g[l, r] - second * (g0[l, r] + first * g1[l, r])
                for r in range(ROWS)
            ],
        )
        send(state.at[l], state_far.at[0, l])
    for copy in copies:
        copy.wait()


VM = pl.BlockSpec(memory_space=pltpu.VMEM)
FARM = pl.BlockSpec(memory_space=pltpu.HBM)


def call(kernel, outs, scratch=(), us=1.0, far_in=False, far_out=False):
    def run(*args):
        if far_in:
            args = [pltpu.with_memory_space_constraint(a, pltpu.HBM) for a in args]
        return pl.pallas_call(
            kernel,
            out_shape=[jax.ShapeDtypeStruct(s, jnp.float32) for s in outs],
            in_specs=[FARM if far_in else VM] * len(args),
            out_specs=[FARM if far_out else VM] * len(outs),
            scratch_shapes=[pltpu.VMEM(s, jnp.float32) if isinstance(s, tuple) else s for s in scratch],
            compiler_params=pltpu.CompilerParams(vmem_limit_bytes=16 * 2**20),
            cost_estimate=pl.CostEstimate(
                flops=int(us * 4e6), bytes_accessed=sum(4 * a.size for a in args), transcendentals=0
            ),
        )(*args)

    return run


def rows_of(k, n):
    return (k, n, *ROW)


def shifted(x, axis, by):
    count = lax.axis_size(axis)
    return lax.ppermute(x, axis, [(i, i + by) for i in range(count) if 0 <= i + by < count])


def both_ways(lows):
    return [p for i in lows for p in ((i, i + 1), (i + 1, i))]


def swapped(one, two):
    count = lax.axis_size(TM)
    return [
        lax.ppermute(x, TM, both_ways(range(start, count - 1, 2))) for x, start in ((one, 1), (two, 0))
    ]


def swapped_rows(x):
    cores, count = lax.axis_size(TM[-1]), lax.axis_size("lat")
    out = []
    for turn in range(2):
        lows = [
            core * count + i for core in range(cores) for i in range((core + turn + 1) % 2, count - 1, 2)
        ]
        out.append(lax.ppermute(x, (TM[-1], "lat"), both_ways(lows)))
    return out


def exchanged(x, axis):
    return lax.all_to_all(x, axis, 0, 0, tiled=True)


def on_device(
    x_init, background, observed, diff_lon, diff_lat, drift, coupling, model_var, obs_level, huber_class
):
    band, wide = rows_of(L, ROWS), rows_of(L, W)
    whole = (L, ROWS, 8 * TILE)
    cells = (ROWS, *ROW)
    two_w = [wide] * 2
    count = float(L * ROWS * 8 * TILE * lax.axis_size(TM) * lax.axis_size("lat"))
    (own,) = call(
        pack_kernel,
        [rows_of(L + 3, ROWS)],
        [whole, (3, *whole[1:]), pltpu.SemaphoreType.DMA((4,))],
        far_in=True,
    )(x_init, diff_lon, diff_lat, drift)
    first, second = swapped_rows(own)
    x, bg, obs, c, keep, level, weight = call(
        aside_kernel, [band, band, cells, (L * L, *ROW), (L, *ROW), cells, cells]
    )(own, background, observed, coupling, model_var[None], obs_level, huber_class)
    after = shifted(x, TM, -1)
    first, second, bg, obs, c, keep, level, weight = lax.optimization_barrier(
        (first, second, bg, obs, c, keep, level, weight)
    )

    three = rows_of(L + 3, ROWS)
    short = [rows_of(L, 3 * H)] * 2
    up, down, moved, *sent = call(forward_kernel, [three, three, band, band, band], two_w)(
        c, first, second, own
    )
    swaps = swapped(*sent)
    (moved_halo,) = call(halo_kernel, [band], short)(c, up, own, down, up, own, down)
    ahead, o1, d, g = call(back_kernel, [wide, cells, band, band], two_w, 1.5)(
        c, *swaps, after, moved, moved_halo, up, own, down, bg, obs, level, weight
    )

    first, second = swapped_rows(g)
    g0, g_copy = call(still_kernel, [band, band], two_w, 1.5)(
        c, keep, d, ahead, up, own, down, level, o1, g
    )
    after_g = shifted(g_copy, TM, -1)
    first, second, g0 = lax.optimization_barrier((first, second, g0))
    up_g, down_g, moved_g, *sent = call(forward_g_kernel, [band] * 5, two_w)(
        c, first, second, g, up, own, down
    )
    swaps = swapped(*sent)
    (moved_g_halo,) = call(halo_kernel, [band], short)(c, up_g, g, down_g, up, own, down)
    u, g1, hg, part = call(
        back_g_kernel,
        [band, band, cells, (lax.axis_size(NEAR), 1, TILE)],
        [wide] + two_w,
        1.5,
    )(c, *swaps, after_g, moved_g, moved_g_halo, up, own, down, g, level, weight, g0)
    (part,) = call(again_kernel, [(lax.axis_size(FAR), 1, TILE)], us=0.1)(exchanged(part, NEAR))
    part = exchanged(part, FAR)

    def finish(*refs):
        last_kernel(count, *refs)

    outs = call(
        finish,
        [(1, *whole), (1, *whole), (1, *whole[1:])],
        [whole, whole, (1, *whole[1:]), pltpu.SemaphoreType.DMA((2 * L + 1,))],
        far_out=True,
    )(part, keep, own, g, g0, g1, d, u, o1, hg)
    return tuple(outs)


def solution(mesh):
    torus = Mesh(mesh.devices.reshape(4, 8, 2, mesh.shape["lat"]), (*TM, "lat"))
    band = P(TM, "lat", None)
    in_specs = (
        P(TM, None, "lat", None),
        P(None, "lat", None),
        band,
        band,
        band,
        band,
        P(),
        P(),
        band,
        band,
    )
    out_specs = (P(TM, None, "lat", None), P(TM, None, "lat", None), band)
    return jax.shard_map(
        on_device, mesh=torus, in_specs=in_specs, out_specs=out_specs, check_vma=False
    )
```

```python
import jax
import jax.numpy as jnp
from jax import lax
from jax.experimental import pallas as pl
from jax.experimental.pallas import tpu as pltpu
from jax.sharding import Mesh
from jax.sharding import PartitionSpec as P

L = 5
TILE = 128
STEPS = 4
ROWS = 8
H = STEPS
W = ROWS + 2 * H
TM = ("tm_0", "tm_1", "tm_2")
FAR = ("tm_0", "tm_1")
NEAR = ("tm_2", "lat")
ROW = (8, TILE)


def lanes():
    return lax.broadcasted_iota(jnp.int32, ROW, 1)


class Shift:
    def __init__(self):
        lane = lanes()
        self.first = lane == 0
        self.last = lane == TILE - 1

    def east(self, v):
        r = pltpu.roll(v, TILE - 1, 1)
        return jnp.where(self.last, pltpu.roll(r, 7, 0), r)

    def west(self, v):
        r = pltpu.roll(v, 1, 1)
        return jnp.where(self.first, pltpu.roll(r, 1, 0), r)


def total(terms):
    while len(terms) > 1:
        terms = [a + b for a, b in zip(terms[::2], terms[1::2])] + (
            [terms[-1]] if len(terms) % 2 else []
        )
    return terms[0]


def centre(ce, cw, ky):
    return (1.0 - (ce + cw)) - 2.0 * ky


def forward(src, coef, c, rows, bufs, dst):
    sh = Shift()
    for step in range(STEPS):
        lo, hi = step + 1, rows - step - 1

        def get(r, step=step):
            if step == 0:
                return [src(l, r) for l in range(L)]
            return [bufs[(step - 1) % 2][l, r] for l in range(L)]

        above, here = get(lo - 1), get(lo)
        for r in range(lo, hi):
            below = get(r + 1)
            ce, cw, ky = coef(0, r), coef(1, r), coef(2, r)
            c0 = centre(ce, cw, ky)
            for l in range(L):
                v = here[l]
                terms = [
                    ce * sh.east(v),
                    cw * sh.west(v),
                    ky * (above[l] + below[l]),
                    c0 * v,
                ] + [c[L * l + m] * here[m] for m in range(L)]
                out = total(terms)
                if step == STEPS - 1:
                    dst(l, r, out)
                else:
                    bufs[step % 2][l, r] = out
            above, here = here, below


def adjoint(src, coef, c, rows, bufs, dst):
    sh = Shift()
    for step in range(STEPS):
        lo, hi = step + 1, rows - step - 1

        def get(r, step=step):
            if step == 0:
                v = [src(l, r) for l in range(L)]
            else:
                v = [bufs[(step - 1) % 2][l, r] for l in range(L)]
            ky = coef(2, r)
            return v, [ky * w for w in v]

        (_, above), (here, q) = get(lo - 1), get(lo)
        for r in range(lo, hi):
            after, below = get(r + 1)
            ce, cw, ky = coef(0, r), coef(1, r), coef(2, r)
            c0 = centre(ce, cw, ky)
            for l in range(L):
                w = here[l]
                terms = [
                    sh.west(ce * w),
                    sh.east(cw * w),
                    above[l] + below[l],
                    c0 * w,
                ] + [c[L * m + l] * here[m] for m in range(L)]
                out = total(terms)
                if step == STEPS - 1:
                    dst(l, r, out)
                else:
                    bufs[step % 2][l, r] = out
            above, here, q = q, after, below


def banded(up, own, down, first):
    def at(k, r):
        part = (up, own, down)[r // ROWS]
        return part[first + k, r % ROWS]

    return at


def place():
    j, n = 0, 1
    for axis in TM:
        j = j * lax.axis_size(axis) + lax.axis_index(axis)
        n = n * lax.axis_size(axis)
    return jnp.where(j == n - 1, 0.0, 1.0), jnp.where(j == 0, 1.0, 0.0)


def split(v):
    return jnp.swapaxes(jnp.stack([v[:, s * TILE : (s + 1) * TILE] for s in range(8)]), 0, 1)


def join_into(ref, index, rows):
    v = jnp.swapaxes(jnp.stack(rows), 0, 1)
    for s in range(8):
        ref[(*index, slice(None), slice(s * TILE, (s + 1) * TILE))] = v[s]


def pack_kernel(x_far, kx_far, ky_far, ux_far, out, x, k3, sems):
    copies = [
        pltpu.make_async_copy(x_far.at[0], x, sems.at[0]),
        pltpu.make_async_copy(kx_far, k3.at[pl.ds(0, 1)], sems.at[1]),
        pltpu.make_async_copy(ky_far, k3.at[pl.ds(1, 1)], sems.at[2]),
        pltpu.make_async_copy(ux_far, k3.at[pl.ds(2, 1)], sems.at[3]),
    ]
    for copy in copies:
        copy.start()
    for copy in copies[1:]:
        copy.wait()
    k, u = k3[0], 0.5 * k3[2]
    out[L] = split(k + u)
    out[L + 1] = split(k - u)
    out[L + 2] = split(k3[1])
    copies[0].wait()
    for l in range(L):
        out[l] = split(x[l])


def tiles(v):
    return jnp.swapaxes(jnp.stack([jnp.broadcast_to(v[:, s : s + 1], ROW) for s in range(8)]), 0, 1)


def aside_kernel(
    own, background, observed, coupling, var, obs_level, huber_class, x, bg, obs, c, keep, level, weight
):
    x[...] = own[:L]
    level[...] = tiles(obs_level[0].astype(jnp.float32))
    h = huber_class[0]
    weight[...] = tiles(jnp.where(h == 0, 1.0, 0.0) + jnp.where(h == 1, 0.5, 0.0) + jnp.where(h == 2, 0.25, 0.0))
    for l in range(L):
        bg[l] = split(background[l])
        keep[l] = jnp.broadcast_to(2.0 - 0.5 * var[:, l : l + 1], ROW)
        for m in range(L):
            c[L * l + m] = jnp.broadcast_to(coupling[l : l + 1, m : m + 1], ROW)
    obs[...] = split(observed[0])


def odd(axis):
    return lax.rem(lax.axis_index(axis), 2) == 1


def sides(first, second, fields, up, down):
    below = lax.rem(lax.axis_index("lat") + lax.axis_index(TM[-1]), 2) == 1
    for k in range(fields):
        for r in range(ROWS):
            up[k, r] = jnp.where(below, second[k, r], first[k, r])
            down[k, r] = jnp.where(below, first[k, r], second[k, r])


def forward_kernel(c, first, second, own, up, down, moved, one, two, a, b):
    sides(first, second, L + 3, up, down)
    send(c, up, own, down, up, own, down, moved, one, two, a, b)


def forward_g_kernel(c, first, second, own, up_c, own_c, down_c, up, down, moved, one, two, a, b):
    sides(first, second, L, up, down)
    send(c, up, own, down, up_c, own_c, down_c, moved, one, two, a, b)


def send(c, up, own, down, up_c, own_c, down_c, moved, one, two, a, b):
    ahead = odd(TM[-1])
    field, coef = banded(up, own, down, 0), banded(up_c, own_c, down_c, L)

    def dst(l, r, v):
        r = r - H
        moved[l, r] = v
        halo = up[l, H + r] if r < H else down[l, r - H]
        one[l, r] = jnp.where(ahead, v, halo)
        two[l, r] = jnp.where(ahead, halo, v)

    forward(lambda l, r: field(l, r + H), lambda k, r: coef(k, r + H), c, W, (a, b), dst)


def halo_kernel(c, up, own, down, up_c, own_c, down_c, moved, a, b):
    field, coef = banded(up, own, down, 0), banded(up_c, own_c, down_c, L)
    for first, to in ((0, 0), (ROWS + H, H)):

        def dst(l, r, v, to=to):
            moved[l, to + r - H] = v

        forward(
            lambda l, r, first=first: field(l, first + r),
            lambda k, r, first=first: coef(k, first + r),
            c,
            3 * H,
            (a, b),
            dst,
        )


def receive(one, two, after, moved, moved_halo, factor, out):
    ahead = odd(TM[-1])
    for l in range(L):
        for r in range(W):
            if H <= r < H + ROWS:
                v = after[l, r - H] - moved[l, r - H]
            else:
                at = r if r < H else r - ROWS
                v = jnp.where(ahead, one[l, at], two[l, at]) - moved_halo[l, at]
            out[l, r] = factor * v
    return lambda l, r: jnp.where(ahead, two[l, r], one[l, r])


def picked(level, values):
    out = jnp.where(level == 0, values[0], 0.0)
    for l in range(1, L):
        out = jnp.where(level == float(l), values[l], out)
    return out


def back_kernel(
    c, one, two, after, moved, moved_halo, up, own, down, bg, obs, level, weight, ahead, o1, d, g, a, b
):
    some, first = place()
    came = receive(one, two, after, moved, moved_halo, 0.5 * some, ahead)
    for r in range(ROWS):
        o1[r] = 0.5 * weight[r] * (picked(level[r], [own[l, r] for l in range(L)]) - obs[r])
    coef = banded(up, own, down, L)

    def dst(l, r, v):
        r = r - H
        one = 0.5 * (own[l, r] - (came(l, r) + first * bg[l, r]))
        d[l, r] = one
        g[l, r] = one - v + jnp.where(level[r] == float(l), o1[r], 0.0)

    adjoint(lambda l, r: ahead[l, r], lambda k, r: coef(k, r + H), c, W, (a, b), dst)


def still_kernel(c, keep, d, ahead, up, own, down, level, o1, g, g0, g_out, a, b):
    g_out[...] = g[...]
    coef = banded(up, own, down, L)

    def dst(l, r, v):
        r = r - H
        g0[l, r] = keep[l] * d[l, r] - v + jnp.where(level[r] == float(l), 1.5 * o1[r], 0.0)

    adjoint(lambda l, r: keep[l] * ahead[l, r], lambda k, r: coef(k, r + H), c, W, (a, b), dst)


def back_g_kernel(
    c, one, two, after, moved, moved_halo, up, own, down, g, level, weight, g0, u, g1, hg, part, ahead, a, b
):
    came = receive(one, two, after, moved, moved_halo, place()[0], ahead)
    for r in range(ROWS):
        hg[r] = weight[r] * picked(level[r], [g[l, r] for l in range(L)])
    coef = banded(up, own, down, L)
    sums = [[], [], [], []]

    def dst(l, r, v):
        r = r - H
        now = g[l, r] - came(l, r)
        u[l, r] = now
        one = -0.5 * (now - v + jnp.where(level[r] == float(l), hg[r], 0.0))
        g1[l, r] = one
        for k, term in enumerate((g[l, r] * g[l, r], g0[l, r] * g0[l, r], g0[l, r] * one, one * one)):
            sums[k].append(term)
            if len(sums[k]) == L:
                sums[k] = [total(sums[k])]

    adjoint(lambda l, r: ahead[l, r], lambda k, r: coef(k, r + H), c, W, (a, b), dst)
    lane = lax.broadcasted_iota(jnp.int32, (1, TILE), 1)
    row = jnp.zeros((1, TILE), jnp.float32)
    for k in range(4):
        s = jnp.sum(jnp.sum(total(sums[k]), axis=0, keepdims=True), axis=1, keepdims=True)
        row = jnp.where(lane == k, s, row)
    for i in range(part.shape[0]):
        part[i] = row


def again_kernel(parts, out):
    s = total([parts[i] for i in range(parts.shape[0])])
    for i in range(out.shape[0]):
        out[i] = s


def last_kernel(
    count, parts, keep, own, g, g0, g1, d, u, o1, hg, state_far, multipliers_far, obs_far, state, multipliers, obs, sems
):
    row = total([parts[i] for i in range(parts.shape[0])])
    lane = lax.broadcasted_iota(jnp.int32, (1, TILE), 1)
    sg, s00, s01, s11 = [
        jnp.broadcast_to(jnp.sum(jnp.where(lane == k, row, 0.0), axis=1, keepdims=True), ROW) / count
        for k in range(4)
    ]
    first = 0.3 / jnp.sqrt(sg + 1e-06)
    mean = jnp.maximum(s00 + first * (2.0 * s01 + first * s11), 0.0)
    second = 0.3 / jnp.sqrt(mean + 1e-06)
    half = 0.5 * first
    copies = []

    def send(here, far):
        copies.append(pltpu.make_async_copy(here, far, sems.at[len(copies)]))
        copies[-1].start()

    join_into(obs, (0,), [1.5 * o1[r] - half * hg[r] for r in range(ROWS)])
    send(obs, obs_far)
    for l in range(L):
        join_into(multipliers, (l,), [keep[l] * d[l, r] - half * u[l, r] for r in range(ROWS)])
        send(multipliers.at[l], multipliers_far.at[0, l])
        join_into(
            state,
            (l,),
            [
                own[l, r] - first * g[l, r] - second * (g0[l, r] + first * g1[l, r])
                for r in range(ROWS)
            ],
        )
        send(state.at[l], state_far.at[0, l])
    for copy in copies:
        copy.wait()


VM = pl.BlockSpec(memory_space=pltpu.VMEM)
FARM = pl.BlockSpec(memory_space=pltpu.HBM)


def call(kernel, outs, scratch=(), us=1.0, far_in=False, far_out=False):
    def run(*args):
        if far_in:
            args = [pltpu.with_memory_space_constraint(a, pltpu.HBM) for a in args]
        return pl.pallas_call(
            kernel,
            out_shape=[jax.ShapeDtypeStruct(s, jnp.float32) for s in outs],
            in_specs=[FARM if far_in else VM] * len(args),
            out_specs=[FARM if far_out else VM] * len(outs),
            scratch_shapes=[pltpu.VMEM(s, jnp.float32) if isinstance(s, tuple) else s for s in scratch],
            compiler_params=pltpu.CompilerParams(vmem_limit_bytes=16 * 2**20),
            cost_estimate=pl.CostEstimate(
                flops=int(us * 4e6), bytes_accessed=sum(4 * a.size for a in args), transcendentals=0
            ),
        )(*args)

    return run


def rows_of(k, n):
    return (k, n, *ROW)


def shifted(x, axis, by):
    count = lax.axis_size(axis)
    return lax.ppermute(x, axis, [(i, i + by) for i in range(count) if 0 <= i + by < count])


def both_ways(lows):
    return [p for i in lows for p in ((i, i + 1), (i + 1, i))]


def swapped(one, two):
    count = lax.axis_size(TM)
    return [
        lax.ppermute(x, TM, both_ways(range(start, count - 1, 2))) for x, start in ((one, 1), (two, 0))
    ]


def swapped_rows(x):
    cores, count = lax.axis_size(TM[-1]), lax.axis_size("lat")
    out = []
    for turn in range(2):
        lows = [
            core * count + i for core in range(cores) for i in range((core + turn + 1) % 2, count - 1, 2)
        ]
        out.append(lax.ppermute(x, (TM[-1], "lat"), both_ways(lows)))
    return out


def exchanged(x, axes):
    order = [0]
    for axis in axes:
        n = lax.axis_size(axis)
        order = [n * i + (k + n // 2) % n for i in order for k in range(n)]
    return lax.all_to_all(x, axes, 0, 0, axis_index_groups=[order], tiled=True)


def on_device(
    x_init, background, observed, diff_lon, diff_lat, drift, coupling, model_var, obs_level, huber_class
):
    band, wide = rows_of(L, ROWS), rows_of(L, W)
    whole = (L, ROWS, 8 * TILE)
    cells = (ROWS, *ROW)
    two_w = [wide] * 2
    count = float(L * ROWS * 8 * TILE * lax.axis_size(TM) * lax.axis_size("lat"))
    (own,) = call(
        pack_kernel,
        [rows_of(L + 3, ROWS)],
        [whole, (3, *whole[1:]), pltpu.SemaphoreType.DMA((4,))],
        far_in=True,
    )(x_init, diff_lon, diff_lat, drift)
    first, second = swapped_rows(own)
    x, bg, obs, c, keep, level, weight = call(
        aside_kernel, [band, band, cells, (L * L, *ROW), (L, *ROW), cells, cells]
    )(own, background, observed, coupling, model_var[None], obs_level, huber_class)
    after = shifted(x, TM, -1)
    first, second, bg, obs, c, keep, level, weight = lax.optimization_barrier(
        (first, second, bg, obs, c, keep, level, weight)
    )

    three = rows_of(L + 3, ROWS)
    short = [rows_of(L, 3 * H)] * 2
    up, down, moved, *sent = call(forward_kernel, [three, three, band, band, band], two_w)(
        c, first, second, own
    )
    swaps = swapped(*sent)
    (moved_halo,) = call(halo_kernel, [band], short)(c, up, own, down, up, own, down)
    ahead, o1, d, g = call(back_kernel, [wide, cells, band, band], two_w, 1.5)(
        c, *swaps, after, moved, moved_halo, up, own, down, bg, obs, level, weight
    )

    first, second = swapped_rows(g)
    g0, g_copy = call(still_kernel, [band, band], two_w, 1.5)(
        c, keep, d, ahead, up, own, down, level, o1, g
    )
    after_g = shifted(g_copy, TM, -1)
    first, second, g0 = lax.optimization_barrier((first, second, g0))
    up_g, down_g, moved_g, *sent = call(forward_g_kernel, [band] * 5, two_w)(
        c, first, second, g, up, own, down
    )
    swaps = swapped(*sent)
    (moved_g_halo,) = call(halo_kernel, [band], short)(c, up_g, g, down_g, up, own, down)
    u, g1, hg, part = call(
        back_g_kernel,
        [band, band, cells, (lax.axis_size(NEAR), 1, TILE)],
        [wide] + two_w,
        1.5,
    )(c, *swaps, after_g, moved_g, moved_g_halo, up, own, down, g, level, weight, g0)
    (part,) = call(again_kernel, [(lax.axis_size(FAR), 1, TILE)], us=0.1)(exchanged(part, NEAR))
    part = exchanged(part, FAR)

    def finish(*refs):
        last_kernel(count, *refs)

    outs = call(
        finish,
        [(1, *whole), (1, *whole), (1, *whole[1:])],
        [whole, whole, (1, *whole[1:]), pltpu.SemaphoreType.DMA((2 * L + 1,))],
        far_out=True,
    )(part, keep, own, g, g0, g1, d, u, o1, hg)
    return tuple(outs)


def solution(mesh):
    torus = Mesh(mesh.devices.reshape(4, 8, 2, mesh.shape["lat"]), (*TM, "lat"))
    band = P(TM, "lat", None)
    in_specs = (
        P(TM, None, "lat", None),
        P(None, "lat", None),
        band,
        band,
        band,
        band,
        P(),
        P(),
        band,
        band,
    )
    out_specs = (P(TM, None, "lat", None), P(TM, None, "lat", None), band)
    return jax.shard_map(
        on_device, mesh=torus, in_specs=in_specs, out_specs=out_specs, check_vma=False
    )
```

```python
import jax
import jax.numpy as jnp
from jax import lax
from jax.experimental import pallas as pl
from jax.experimental.pallas import tpu as pltpu
from jax.sharding import Mesh
from jax.sharding import PartitionSpec as P

L = 5
TILE = 128
STEPS = 4
ROWS = 8
H = STEPS
W = ROWS + 2 * H
TM = ("tm_0", "tm_1", "tm_2")
FAR = ("tm_0", "tm_1")
NEAR = ("tm_2", "lat")
ROW = (8, TILE)


def lanes():
    return lax.broadcasted_iota(jnp.int32, ROW, 1)


class Shift:
    def __init__(self):
        lane = lanes()
        self.first = lane == 0
        self.last = lane == TILE - 1

    def east(self, v):
        r = pltpu.roll(v, TILE - 1, 1)
        return jnp.where(self.last, pltpu.roll(r, 7, 0), r)

    def west(self, v):
        r = pltpu.roll(v, 1, 1)
        return jnp.where(self.first, pltpu.roll(r, 1, 0), r)


def total(terms):
    while len(terms) > 1:
        terms = [a + b for a, b in zip(terms[::2], terms[1::2])] + (
            [terms[-1]] if len(terms) % 2 else []
        )
    return terms[0]


def centre(ce, cw, ky):
    return (1.0 - (ce + cw)) - 2.0 * ky


def inside(step):
    return range(H + 1 + step, H + ROWS - 1 - step)


INNER = sum(len(inside(step)) for step in range(STEPS))


def slot(step, r):
    return sum(len(inside(s)) for s in range(step)) + r - inside(step)[0]


def march(row, src, rows, bufs, dst, inner, fill):
    for step in range(STEPS):
        lo, hi = step + 1, rows - step - 1
        if fill:
            lo, hi = inside(step).start, inside(step).stop
        ready = inside(step) if inner is not None and not fill else ()

        def get(l, r, step=step):
            if step == 0:
                return src(l, r)
            if inner is not None and r in inside(step - 1):
                return inner[l, slot(step - 1, r)]
            return bufs[(step - 1) % 2][l, r]

        for r in range(lo, hi):
            if r in ready:
                continue
            for l, out in enumerate(row(get, r)):
                if fill:
                    inner[l, slot(step, r)] = out
                elif step == STEPS - 1:
                    dst(l, r, out)
                else:
                    bufs[step % 2][l, r] = out


def forward(src, coef, c, rows, bufs, dst, inner=None, fill=False):
    sh = Shift()

    def row(get, r):
        above, here, below = [[get(l, at) for l in range(L)] for at in (r - 1, r, r + 1)]
        ce, cw, ky = coef(0, r), coef(1, r), coef(2, r)
        c0 = centre(ce, cw, ky)
        for l in range(L):
            v = here[l]
            yield total(
                [ce * sh.east(v), cw * sh.west(v), ky * (above[l] + below[l]), c0 * v]
                + [c[L * l + m] * here[m] for m in range(L)]
            )

    march(row, src, rows, bufs, dst, inner, fill)


def adjoint(src, coef, c, rows, bufs, dst, inner=None, fill=False):
    sh = Shift()

    def row(get, r):
        above, here, below = [[get(l, at) for l in range(L)] for at in (r - 1, r, r + 1)]
        ce, cw, ky = coef(0, r), coef(1, r), coef(2, r)
        ky_above, ky_below = coef(2, r - 1), coef(2, r + 1)
        c0 = centre(ce, cw, ky)
        for l in range(L):
            w = here[l]
            yield total(
                [
                    sh.west(ce * w),
                    sh.east(cw * w),
                    ky_above * above[l] + ky_below * below[l],
                    c0 * w,
                ]
                + [c[L * m + l] * here[m] for m in range(L)]
            )

    march(row, src, rows, bufs, dst, inner, fill)


def banded(up, own, down, first):
    def at(k, r):
        part = (up, own, down)[r // ROWS]
        return part[first + k, r % ROWS]

    return at


def place():
    j, n = 0, 1
    for axis in TM:
        j = j * lax.axis_size(axis) + lax.axis_index(axis)
        n = n * lax.axis_size(axis)
    return jnp.where(j == n - 1, 0.0, 1.0), jnp.where(j == 0, 1.0, 0.0)


def split(v):
    return jnp.swapaxes(jnp.stack([v[:, s * TILE : (s + 1) * TILE] for s in range(8)]), 0, 1)


def join_into(ref, index, rows):
    v = jnp.swapaxes(jnp.stack(rows), 0, 1)
    for s in range(8):
        ref[(*index, slice(None), slice(s * TILE, (s + 1) * TILE))] = v[s]


def pack_kernel(x_far, kx_far, ky_far, ux_far, out, x, k3, sems):
    copies = [
        pltpu.make_async_copy(x_far.at[0], x, sems.at[0]),
        pltpu.make_async_copy(kx_far, k3.at[pl.ds(0, 1)], sems.at[1]),
        pltpu.make_async_copy(ky_far, k3.at[pl.ds(1, 1)], sems.at[2]),
        pltpu.make_async_copy(ux_far, k3.at[pl.ds(2, 1)], sems.at[3]),
    ]
    for copy in copies:
        copy.start()
    for copy in copies[1:]:
        copy.wait()
    k, u = k3[0], 0.5 * k3[2]
    out[L] = split(k + u)
    out[L + 1] = split(k - u)
    out[L + 2] = split(k3[1])
    copies[0].wait()
    for l in range(L):
        out[l] = split(x[l])


def tiles(v):
    return jnp.swapaxes(jnp.stack([jnp.broadcast_to(v[:, s : s + 1], ROW) for s in range(8)]), 0, 1)


def aside_kernel(
    own, background, observed, coupling, var, obs_level, huber_class, x, bg, obs, c, keep, level, weight
):
    x[...] = own[:L]
    level[...] = tiles(obs_level[0].astype(jnp.float32))
    h = huber_class[0]
    weight[...] = tiles(jnp.where(h == 0, 1.0, 0.0) + jnp.where(h == 1, 0.5, 0.0) + jnp.where(h == 2, 0.25, 0.0))
    for l in range(L):
        bg[l] = split(background[l])
        keep[l] = jnp.broadcast_to(2.0 - 0.5 * var[:, l : l + 1], ROW)
        for m in range(L):
            c[L * l + m] = jnp.broadcast_to(coupling[l : l + 1, m : m + 1], ROW)
    obs[...] = split(observed[0])


def odd(axis):
    return lax.rem(lax.axis_index(axis), 2) == 1


def sides(first, second, fields, up, down):
    below = lax.rem(lax.axis_index("lat") + lax.axis_index(TM[-1]), 2) == 1
    for k in range(fields):
        for r in range(ROWS):
            up[k, r] = jnp.where(below, second[k, r], first[k, r])
            down[k, r] = jnp.where(below, first[k, r], second[k, r])


def forward_kernel(c, first, second, own, inner, up, down, moved, one, two, a, b):
    sides(first, second, L + 3, up, down)
    send(c, up, own, down, up, own, down, inner, moved, one, two, a, b)


def forward_g_kernel(
    c, first, second, own, up_c, own_c, down_c, inner, up, down, moved, one, two, a, b
):
    sides(first, second, L, up, down)
    send(c, up, own, down, up_c, own_c, down_c, inner, moved, one, two, a, b)


def send(c, up, own, down, up_c, own_c, down_c, inner, moved, one, two, a, b):
    ahead = odd(TM[-1])
    field, coef = banded(up, own, down, 0), banded(up_c, own_c, down_c, L)

    def dst(l, r, v):
        r = r - H
        moved[l, r] = v
        halo = up[l, H + r] if r < H else down[l, r - H]
        one[l, r] = jnp.where(ahead, v, halo)
        two[l, r] = jnp.where(ahead, halo, v)

    forward(lambda l, r: field(l, r + H), lambda k, r: coef(k, r + H), c, W, (a, b), dst, inner)


def halo_kernel(
    factor, c, after, moved, up, own, down, up_c, own_c, down_c, moved_halo, ahead, inner, a, b
):
    field, coef = banded(up, own, down, 0), banded(up_c, own_c, down_c, L)
    for first, to in ((0, 0), (ROWS + H, H)):

        def dst(l, r, v, to=to):
            moved_halo[l, to + r - H] = v

        forward(
            lambda l, r, first=first: field(l, first + r),
            lambda k, r, first=first: coef(k, first + r),
            c,
            3 * H,
            (a, b),
            dst,
        )
    factor = factor * place()[0]
    for l in range(L):
        for r in range(ROWS):
            ahead[l, r] = factor * (after[l, r] - moved[l, r])
    adjoint(
        lambda l, r: ahead[l, r - H], lambda k, r: own_c[L + k, r - H], c, W, None, None, inner, True
    )


def receive(factor, one, two, ahead, moved_halo):
    odd_one = odd(TM[-1])
    factor = factor * place()[0]

    def next_one(l, r):
        if H <= r < H + ROWS:
            return ahead[l, r - H]
        at = r if r < H else r - ROWS
        return factor * (jnp.where(odd_one, one[l, at], two[l, at]) - moved_halo[l, at])

    return next_one, lambda l, r: jnp.where(odd_one, two[l, r], one[l, r])


def picked(level, values):
    out = jnp.where(level == 0, values[0], 0.0)
    for l in range(1, L):
        out = jnp.where(level == float(l), values[l], out)
    return out


def early_kernel(c, own, obs, level, weight, o1, inner):
    for r in range(ROWS):
        o1[r] = 0.5 * weight[r] * (picked(level[r], [own[l, r] for l in range(L)]) - obs[r])
    forward(
        lambda l, r: own[l, r - H], lambda k, r: own[L + k, r - H], c, W, None, None, inner, True
    )


def back_kernel(
    c, one, two, ahead_own, moved_halo, inner, up, own, down, bg, level, o1, ahead, d, g, a, b
):
    first = place()[1]
    next_one, came = receive(0.5, one, two, ahead_own, moved_halo)
    for l in range(L):
        for r in range(W):
            ahead[l, r] = next_one(l, r)
    coef = banded(up, own, down, L)

    def dst(l, r, v):
        r = r - H
        now = 0.5 * (own[l, r] - (came(l, r) + first * bg[l, r]))
        d[l, r] = now
        g[l, r] = now - v + jnp.where(level[r] == float(l), o1[r], 0.0)

    adjoint(lambda l, r: ahead[l, r], lambda k, r: coef(k, r + H), c, W, (a, b), dst, inner)


def still_kernel(
    c, keep, d, ahead, up, own, down, level, weight, o1, g, g0, g_out, hg, inner, early, a, b
):
    g_out[...] = g[...]
    for r in range(ROWS):
        hg[r] = weight[r] * picked(level[r], [g[l, r] for l in range(L)])
    forward(
        lambda l, r: g[l, r - H], lambda k, r: own[L + k, r - H], c, W, None, None, inner, True
    )
    coef = banded(up, own, down, L)
    sums = []

    def dst(l, r, v):
        r = r - H
        now = keep[l] * d[l, r] - v + jnp.where(level[r] == float(l), 1.5 * o1[r], 0.0)
        g0[l, r] = now
        sums.append(now * now)

    adjoint(lambda l, r: keep[l] * ahead[l, r], lambda k, r: coef(k, r + H), c, W, (a, b), dst)
    early[0] = total([g[l, r] * g[l, r] for l in range(L) for r in range(ROWS)])
    early[1] = total(sums)


def back_g_kernel(
    c, one, two, ahead_own, moved_halo, inner, up, own, down, g, level, hg, g0, early, u, g1, part, ahead, a, b
):
    next_one, came = receive(1.0, one, two, ahead_own, moved_halo)
    for l in range(L):
        for r in range(W):
            ahead[l, r] = next_one(l, r)
    coef = banded(up, own, down, L)
    late = [[], []]

    def dst(l, r, v):
        r = r - H
        now = g[l, r] - came(l, r)
        u[l, r] = now
        one = -0.5 * (now - v + jnp.where(level[r] == float(l), hg[r], 0.0))
        g1[l, r] = one
        for k, term in enumerate((g0[l, r] * one, one * one)):
            late[k].append(term)
            if len(late[k]) == L:
                late[k] = [total(late[k])]

    adjoint(lambda l, r: ahead[l, r], lambda k, r: coef(k, r + H), c, W, (a, b), dst, inner)
    lane = lax.broadcasted_iota(jnp.int32, (1, TILE), 1)
    row = jnp.zeros((1, TILE), jnp.float32)
    for k, v in enumerate((early[0], early[1], total(late[0]), total(late[1]))):
        s = jnp.sum(jnp.sum(v, axis=0, keepdims=True), axis=1, keepdims=True)
        row = jnp.where(lane == k, s, row)
    for i in range(part.shape[0]):
        part[i] = row


def again_kernel(parts, out):
    s = total([parts[i] for i in range(parts.shape[0])])
    for i in range(out.shape[0]):
        out[i] = s


def last_kernel(
    count, parts, keep, own, g, g0, g1, d, u, o1, hg, state_far, multipliers_far, obs_far, state, multipliers, obs, sems
):
    row = total([parts[i] for i in range(parts.shape[0])])
    lane = lax.broadcasted_iota(jnp.int32, (1, TILE), 1)
    sg, s00, s01, s11 = [
        jnp.broadcast_to(jnp.sum(jnp.where(lane == k, row, 0.0), axis=1, keepdims=True), ROW) / count
        for k in range(4)
    ]
    first = 0.3 / jnp.sqrt(sg + 1e-06)
    mean = jnp.maximum(s00 + first * (2.0 * s01 + first * s11), 0.0)
    second = 0.3 / jnp.sqrt(mean + 1e-06)
    half = 0.5 * first
    copies = []

    def send(here, far):
        copies.append(pltpu.make_async_copy(here, far, sems.at[len(copies)]))
        copies[-1].start()

    join_into(obs, (0,), [1.5 * o1[r] - half * hg[r] for r in range(ROWS)])
    send(obs, obs_far)
    for l in range(L):
        join_into(multipliers, (l,), [keep[l] * d[l, r] - half * u[l, r] for r in range(ROWS)])
        send(multipliers.at[l], multipliers_far.at[0, l])
        join_into(
            state,
            (l,),
            [
                own[l, r] - first * g[l, r] - second * (g0[l, r] + first * g1[l, r])
                for r in range(ROWS)
            ],
        )
        send(state.at[l], state_far.at[0, l])
    for copy in copies:
        copy.wait()


VM = pl.BlockSpec(memory_space=pltpu.VMEM)
FARM = pl.BlockSpec(memory_space=pltpu.HBM)


def call(kernel, outs, scratch=(), us=1.0, far_in=False, far_out=False):
    def run(*args):
        if far_in:
            args = [pltpu.with_memory_space_constraint(a, pltpu.HBM) for a in args]
        return pl.pallas_call(
            kernel,
            out_shape=[jax.ShapeDtypeStruct(s, jnp.float32) for s in outs],
            in_specs=[FARM if far_in else VM] * len(args),
            out_specs=[FARM if far_out else VM] * len(outs),
            scratch_shapes=[pltpu.VMEM(s, jnp.float32) if isinstance(s, tuple) else s for s in scratch],
            compiler_params=pltpu.CompilerParams(vmem_limit_bytes=16 * 2**20),
            cost_estimate=pl.CostEstimate(
                flops=int(us * 4e6), bytes_accessed=sum(4 * a.size for a in args), transcendentals=0
            ),
        )(*args)

    return run


def rows_of(k, n):
    return (k, n, *ROW)


def shifted(x, axis, by):
    count = lax.axis_size(axis)
    return lax.ppermute(x, axis, [(i, i + by) for i in range(count) if 0 <= i + by < count])


def both_ways(lows):
    return [p for i in lows for p in ((i, i + 1), (i + 1, i))]


def swapped(one, two):
    count = lax.axis_size(TM)
    return [
        lax.ppermute(x, TM, both_ways(range(start, count - 1, 2))) for x, start in ((one, 1), (two, 0))
    ]


def swapped_rows(x):
    cores, count = lax.axis_size(TM[-1]), lax.axis_size("lat")
    out = []
    for turn in range(2):
        lows = [
            core * count + i for core in range(cores) for i in range((core + turn + 1) % 2, count - 1, 2)
        ]
        out.append(lax.ppermute(x, (TM[-1], "lat"), both_ways(lows)))
    return out


def exchanged(x, axes):
    order = [0]
    for axis in axes:
        n = lax.axis_size(axis)
        order = [n * i + (k + n // 2) % n for i in order for k in range(n)]
    return lax.all_to_all(x, axes, 0, 0, axis_index_groups=[order], tiled=True)


def on_device(
    x_init, background, observed, diff_lon, diff_lat, drift, coupling, model_var, obs_level, huber_class
):
    band, wide = rows_of(L, ROWS), rows_of(L, W)
    whole = (L, ROWS, 8 * TILE)
    cells = (ROWS, *ROW)
    two_w = [wide] * 2
    count = float(L * ROWS * 8 * TILE * lax.axis_size(TM) * lax.axis_size("lat"))
    (own,) = call(
        pack_kernel,
        [rows_of(L + 3, ROWS)],
        [whole, (3, *whole[1:]), pltpu.SemaphoreType.DMA((4,))],
        far_in=True,
    )(x_init, diff_lon, diff_lat, drift)
    first, second = swapped_rows(own)
    x, bg, obs, c, keep, level, weight = call(
        aside_kernel, [band, band, cells, (L * L, *ROW), (L, *ROW), cells, cells]
    )(own, background, observed, coupling, model_var[None], obs_level, huber_class)
    after = shifted(x, TM, -1)
    inside_rows = rows_of(L, INNER)
    o1, inner = call(early_kernel, [cells, inside_rows], us=0.5)(c, own, obs, level, weight)
    first, second, bg, keep, o1, inner = lax.optimization_barrier(
        (first, second, bg, keep, o1, inner)
    )

    def half_way(factor):
        return call(
            lambda *refs: halo_kernel(factor, *refs), [band, band, inside_rows], [rows_of(L, 3 * H)] * 2
        )

    three = rows_of(L + 3, ROWS)
    up, down, moved, *sent = call(forward_kernel, [three, three, band, band, band], two_w)(
        c, first, second, own, inner
    )
    swaps = swapped(*sent)
    moved_halo, ahead_own, inner = half_way(0.5)(c, after, moved, up, own, down, up, own, down)
    *swaps, moved_halo = lax.optimization_barrier((*swaps, moved_halo))
    ahead, d, g = call(back_kernel, [wide, band, band], two_w)(
        c, *swaps, ahead_own, moved_halo, inner, up, own, down, bg, level, o1
    )

    first, second = swapped_rows(g)
    g0, g_copy, hg, inner, early = call(
        still_kernel, [band, band, cells, inside_rows, (2, *ROW)], two_w, 1.5
    )(c, keep, d, ahead, up, own, down, level, weight, o1, g)
    after_g = shifted(g_copy, TM, -1)
    first, second, g0 = lax.optimization_barrier((first, second, g0))
    up_g, down_g, moved_g, *sent = call(forward_g_kernel, [band] * 5, two_w)(
        c, first, second, g, up, own, down, inner
    )
    swaps = swapped(*sent)
    moved_halo, ahead_own, inner = half_way(1.0)(
        c, after_g, moved_g, up_g, g, down_g, up, own, down
    )
    *swaps, moved_halo = lax.optimization_barrier((*swaps, moved_halo))
    u, g1, part = call(
        back_g_kernel, [band, band, (lax.axis_size(NEAR), 1, TILE)], [wide] + two_w
    )(c, *swaps, ahead_own, moved_halo, inner, up, own, down, g, level, hg, g0, early)
    (part,) = call(again_kernel, [(lax.axis_size(FAR), 1, TILE)], us=0.1)(exchanged(part, NEAR))
    part = exchanged(part, FAR)

    def finish(*refs):
        last_kernel(count, *refs)

    outs = call(
        finish,
        [(1, *whole), (1, *whole), (1, *whole[1:])],
        [whole, whole, (1, *whole[1:]), pltpu.SemaphoreType.DMA((2 * L + 1,))],
        far_out=True,
    )(part, keep, own, g, g0, g1, d, u, o1, hg)
    return tuple(outs)


def solution(mesh):
    torus = Mesh(mesh.devices.reshape(4, 8, 2, mesh.shape["lat"]), (*TM, "lat"))
    band = P(TM, "lat", None)
    in_specs = (
        P(TM, None, "lat", None),
        P(None, "lat", None),
        band,
        band,
        band,
        band,
        P(),
        P(),
        band,
        band,
    )
    out_specs = (P(TM, None, "lat", None), P(TM, None, "lat", None), band)
    return jax.shard_map(
        on_device, mesh=torus, in_specs=in_specs, out_specs=out_specs, check_vma=False
    )
```

```python
import jax
import jax.numpy as jnp
from jax import lax
from jax.experimental import pallas as pl
from jax.experimental.pallas import tpu as pltpu
from jax.sharding import Mesh
from jax.sharding import PartitionSpec as P

L = 5
TILE = 128
STEPS = 4
ROWS = 8
H = STEPS
W = ROWS + 2 * H
TM = ("tm_0", "tm_1", "tm_2")
FAR = ("tm_0", "tm_1")
NEAR = ("tm_2", "lat")
ROW = (8, TILE)


def lanes():
    return lax.broadcasted_iota(jnp.int32, ROW, 1)


class Shift:
    def __init__(self):
        lane = lanes()
        self.first = lane == 0
        self.last = lane == TILE - 1

    def east(self, v):
        r = pltpu.roll(v, TILE - 1, 1)
        return jnp.where(self.last, pltpu.roll(r, 7, 0), r)

    def west(self, v):
        r = pltpu.roll(v, 1, 1)
        return jnp.where(self.first, pltpu.roll(r, 1, 0), r)


def total(terms):
    while len(terms) > 1:
        terms = [a + b for a, b in zip(terms[::2], terms[1::2])] + (
            [terms[-1]] if len(terms) % 2 else []
        )
    return terms[0]


def centre(ce, cw, ky):
    return (1.0 - (ce + cw)) - 2.0 * ky


def inside(step):
    return range(H + 1 + step, H + ROWS - 1 - step)


INNER = sum(len(inside(step)) for step in range(STEPS))


def slot(step, r):
    return sum(len(inside(s)) for s in range(step)) + r - inside(step)[0]


class Once:
    def __init__(self, of):
        self.of, self.kept = of, {}

    def __call__(self, l, r, name=None, make=None):
        key = (name, l, r)
        if key not in self.kept:
            self.kept[key] = self.of(l, r) if make is None else make()
        return self.kept[key]


def march(row, src, rows, bufs, dst, inner, fill):
    for step in range(STEPS):
        lo, hi = step + 1, rows - step - 1
        if fill:
            lo, hi = inside(step).start, inside(step).stop
        ready = inside(step) if inner is not None and not fill else ()

        def load(l, r, step=step):
            if step == 0:
                return src(l, r)
            if inner is not None and r in inside(step - 1):
                return inner[l, slot(step - 1, r)]
            return bufs[(step - 1) % 2][l, r]

        get = Once(load)

        for r in range(lo, hi):
            if r in ready:
                continue
            for l, out in enumerate(row(get, r)):
                if fill:
                    inner[l, slot(step, r)] = out
                elif step == STEPS - 1:
                    dst(l, r, out)
                else:
                    bufs[step % 2][l, r] = out


def forward(src, coef, c, rows, bufs, dst, inner=None, fill=False):
    sh = Shift()

    def row(get, r):
        above, here, below = [[get(l, at) for l in range(L)] for at in (r - 1, r, r + 1)]
        ce, cw, ky = coef(0, r), coef(1, r), coef(2, r)
        c0 = centre(ce, cw, ky)
        for l in range(L):
            v = here[l]
            yield total(
                [ce * sh.east(v), cw * sh.west(v), ky * (above[l] + below[l]), (c0 + c[(L + 1) * l]) * v]
                + [c[L * l + m] * here[m] for m in range(L) if m != l]
            )

    march(row, src, rows, bufs, dst, inner, fill)


def adjoint(src, coef, c, rows, bufs, dst, inner=None, fill=False):
    sh = Shift()

    def row(get, r):
        here = [get(l, r) for l in range(L)]
        ce, cw, ky = coef(0, r), coef(1, r), coef(2, r)

        def flux(l, r):
            return get(l, r, "ky", lambda: coef(2, r) * get(l, r))

        c0 = centre(ce, cw, ky)
        for l in range(L):
            w = here[l]
            yield total(
                [
                    sh.west(ce * w),
                    sh.east(cw * w),
                    flux(l, r - 1) + flux(l, r + 1),
                    (c0 + c[(L + 1) * l]) * w,
                ]
                + [c[L * m + l] * here[m] for m in range(L) if m != l]
            )

    march(row, src, rows, bufs, dst, inner, fill)


def banded(up, own, down, first):
    def at(k, r):
        part = (up, own, down)[r // ROWS]
        return part[first + k, r % ROWS]

    return at


def place():
    j, n = 0, 1
    for axis in TM:
        j = j * lax.axis_size(axis) + lax.axis_index(axis)
        n = n * lax.axis_size(axis)
    return jnp.where(j == n - 1, 0.0, 1.0), jnp.where(j == 0, 1.0, 0.0)


def split(v):
    return jnp.swapaxes(jnp.stack([v[:, s * TILE : (s + 1) * TILE] for s in range(8)]), 0, 1)


def join_into(ref, index, rows):
    v = jnp.swapaxes(jnp.stack(rows), 0, 1)
    for s in range(8):
        ref[(*index, slice(None), slice(s * TILE, (s + 1) * TILE))] = v[s]


def pack_kernel(x_far, kx_far, ky_far, ux_far, out, x, k3, sems):
    copies = [
        pltpu.make_async_copy(x_far.at[0], x, sems.at[0]),
        pltpu.make_async_copy(kx_far, k3.at[pl.ds(0, 1)], sems.at[1]),
        pltpu.make_async_copy(ky_far, k3.at[pl.ds(1, 1)], sems.at[2]),
        pltpu.make_async_copy(ux_far, k3.at[pl.ds(2, 1)], sems.at[3]),
    ]
    for copy in copies:
        copy.start()
    for copy in copies[1:]:
        copy.wait()
    k, u = k3[0], 0.5 * k3[2]
    out[L] = split(k + u)
    out[L + 1] = split(k - u)
    out[L + 2] = split(k3[1])
    copies[0].wait()
    for l in range(L):
        out[l] = split(x[l])


def tiles(v):
    return jnp.swapaxes(jnp.stack([jnp.broadcast_to(v[:, s : s + 1], ROW) for s in range(8)]), 0, 1)


def aside_kernel(
    own, background, observed, coupling, var, obs_level, huber_class, x, bg, obs, c, keep, level, weight
):
    x[...] = own[:L]
    level[...] = tiles(obs_level[0].astype(jnp.float32))
    h = huber_class[0]
    weight[...] = tiles(jnp.where(h == 0, 1.0, 0.0) + jnp.where(h == 1, 0.5, 0.0) + jnp.where(h == 2, 0.25, 0.0))
    for l in range(L):
        bg[l] = split(background[l])
        keep[l] = jnp.broadcast_to(2.0 - 0.5 * var[:, l : l + 1], ROW)
        for m in range(L):
            c[L * l + m] = jnp.broadcast_to(coupling[l : l + 1, m : m + 1], ROW)
    obs[...] = split(observed[0])


def odd(axis):
    return lax.rem(lax.axis_index(axis), 2) == 1


def sides(first, second, fields, up, down):
    below = lax.rem(lax.axis_index("lat") + lax.axis_index(TM[-1]), 2) == 1
    for k in range(fields):
        for r in range(ROWS):
            up[k, r] = jnp.where(below, second[k, r], first[k, r])
            down[k, r] = jnp.where(below, first[k, r], second[k, r])


def forward_kernel(c, first, second, own, inner, up, down, moved, one, two, a, b):
    sides(first, second, L + 3, up, down)
    send(c, up, own, down, up, own, down, inner, moved, one, two, a, b)


def forward_g_kernel(
    c, first, second, own, up_c, own_c, down_c, inner, up, down, moved, one, two, a, b
):
    sides(first, second, L, up, down)
    send(c, up, own, down, up_c, own_c, down_c, inner, moved, one, two, a, b)


def send(c, up, own, down, up_c, own_c, down_c, inner, moved, one, two, a, b):
    ahead = odd(TM[-1])
    field, coef = banded(up, own, down, 0), banded(up_c, own_c, down_c, L)

    def dst(l, r, v):
        r = r - H
        moved[l, r] = v
        halo = up[l, H + r] if r < H else down[l, r - H]
        one[l, r] = jnp.where(ahead, v, halo)
        two[l, r] = jnp.where(ahead, halo, v)

    forward(lambda l, r: field(l, r + H), lambda k, r: coef(k, r + H), c, W, (a, b), dst, inner)


def halo_kernel(
    factor, c, after, moved, up, own, down, up_c, own_c, down_c, moved_halo, ahead, inner, a, b
):
    field, coef = banded(up, own, down, 0), banded(up_c, own_c, down_c, L)
    for first, to in ((0, 0), (ROWS + H, H)):

        def dst(l, r, v, to=to):
            moved_halo[l, to + r - H] = v

        forward(
            lambda l, r, first=first: field(l, first + r),
            lambda k, r, first=first: coef(k, first + r),
            c,
            3 * H,
            (a, b),
            dst,
        )
    factor = factor * place()[0]
    for l in range(L):
        for r in range(ROWS):
            ahead[l, r] = factor * (after[l, r] - moved[l, r])
    adjoint(
        lambda l, r: ahead[l, r - H], lambda k, r: own_c[L + k, r - H], c, W, None, None, inner, True
    )


def receive(factor, one, two, ahead, moved_halo):
    odd_one = odd(TM[-1])
    factor = factor * place()[0]

    def next_one(l, r):
        if H <= r < H + ROWS:
            return ahead[l, r - H]
        at = r if r < H else r - ROWS
        return factor * (jnp.where(odd_one, one[l, at], two[l, at]) - moved_halo[l, at])

    return next_one, lambda l, r: jnp.where(odd_one, two[l, r], one[l, r])


def picked(level, values):
    out = jnp.where(level == 0, values[0], 0.0)
    for l in range(1, L):
        out = jnp.where(level == float(l), values[l], out)
    return out


def early_kernel(c, own, obs, level, weight, o1, inner):
    for r in range(ROWS):
        o1[r] = 0.5 * weight[r] * (picked(level[r], [own[l, r] for l in range(L)]) - obs[r])
    forward(
        lambda l, r: own[l, r - H], lambda k, r: own[L + k, r - H], c, W, None, None, inner, True
    )


def back_kernel(
    c, one, two, ahead_own, moved_halo, inner, up, own, down, bg, level, o1, ahead, d, g, a, b
):
    first = place()[1]
    next_one, came = receive(0.5, one, two, ahead_own, moved_halo)
    for l in range(L):
        for r in range(W):
            ahead[l, r] = next_one(l, r)
    coef = banded(up, own, down, L)

    def dst(l, r, v):
        r = r - H
        now = 0.5 * (own[l, r] - (came(l, r) + first * bg[l, r]))
        d[l, r] = now
        g[l, r] = now - v + jnp.where(level[r] == float(l), o1[r], 0.0)

    adjoint(lambda l, r: ahead[l, r], lambda k, r: coef(k, r + H), c, W, (a, b), dst, inner)


def still_kernel(
    c, keep, d, ahead, up, own, down, level, weight, o1, g, g0, g_out, hg, inner, early, a, b
):
    g_out[...] = g[...]
    for r in range(ROWS):
        hg[r] = weight[r] * picked(level[r], [g[l, r] for l in range(L)])
    forward(
        lambda l, r: g[l, r - H], lambda k, r: own[L + k, r - H], c, W, None, None, inner, True
    )
    coef = banded(up, own, down, L)
    sums = []

    def dst(l, r, v):
        r = r - H
        now = keep[l] * d[l, r] - v + jnp.where(level[r] == float(l), 1.5 * o1[r], 0.0)
        g0[l, r] = now
        sums.append(now * now)

    adjoint(lambda l, r: keep[l] * ahead[l, r], lambda k, r: coef(k, r + H), c, W, (a, b), dst)
    early[0] = total([g[l, r] * g[l, r] for l in range(L) for r in range(ROWS)])
    early[1] = total(sums)


def back_g_kernel(
    c, one, two, ahead_own, moved_halo, inner, up, own, down, g, level, hg, g0, early, u, g1, part, ahead, a, b
):
    next_one, came = receive(1.0, one, two, ahead_own, moved_halo)
    for l in range(L):
        for r in range(W):
            ahead[l, r] = next_one(l, r)
    coef = banded(up, own, down, L)
    late = [[], []]

    def dst(l, r, v):
        r = r - H
        now = g[l, r] - came(l, r)
        u[l, r] = now
        one = -0.5 * (now - v + jnp.where(level[r] == float(l), hg[r], 0.0))
        g1[l, r] = one
        for k, term in enumerate((g0[l, r] * one, one * one)):
            late[k].append(term)
            if len(late[k]) == L:
                late[k] = [total(late[k])]

    adjoint(lambda l, r: ahead[l, r], lambda k, r: coef(k, r + H), c, W, (a, b), dst, inner)
    lane = lax.broadcasted_iota(jnp.int32, (1, TILE), 1)
    row = jnp.zeros((1, TILE), jnp.float32)
    for k, v in enumerate((early[0], early[1], total(late[0]), total(late[1]))):
        s = jnp.sum(jnp.sum(v, axis=0, keepdims=True), axis=1, keepdims=True)
        row = jnp.where(lane == k, s, row)
    for i in range(part.shape[0]):
        part[i] = row


def again_kernel(parts, out):
    s = total([parts[i] for i in range(parts.shape[0])])
    for i in range(out.shape[0]):
        out[i] = s


def last_kernel(
    count, parts, keep, own, g, g0, g1, d, u, o1, hg, state_far, multipliers_far, obs_far, state, multipliers, obs, sems
):
    row = total([parts[i] for i in range(parts.shape[0])])
    lane = lax.broadcasted_iota(jnp.int32, (1, TILE), 1)
    sg, s00, s01, s11 = [
        jnp.broadcast_to(jnp.sum(jnp.where(lane == k, row, 0.0), axis=1, keepdims=True), ROW) / count
        for k in range(4)
    ]
    first = 0.3 / jnp.sqrt(sg + 1e-06)
    mean = jnp.maximum(s00 + first * (2.0 * s01 + first * s11), 0.0)
    second = 0.3 / jnp.sqrt(mean + 1e-06)
    half = 0.5 * first
    copies = []

    def send(here, far):
        copies.append(pltpu.make_async_copy(here, far, sems.at[len(copies)]))
        copies[-1].start()

    join_into(obs, (0,), [1.5 * o1[r] - half * hg[r] for r in range(ROWS)])
    send(obs, obs_far)
    for l in range(L):
        join_into(multipliers, (l,), [keep[l] * d[l, r] - half * u[l, r] for r in range(ROWS)])
        send(multipliers.at[l], multipliers_far.at[0, l])
        join_into(
            state,
            (l,),
            [
                own[l, r] - first * g[l, r] - second * (g0[l, r] + first * g1[l, r])
                for r in range(ROWS)
            ],
        )
        send(state.at[l], state_far.at[0, l])
    for copy in copies:
        copy.wait()


VM = pl.BlockSpec(memory_space=pltpu.VMEM)
FARM = pl.BlockSpec(memory_space=pltpu.HBM)


def call(kernel, outs, scratch=(), us=1.0, far_in=False, far_out=False):
    def run(*args):
        if far_in:
            args = [pltpu.with_memory_space_constraint(a, pltpu.HBM) for a in args]
        return pl.pallas_call(
            kernel,
            out_shape=[jax.ShapeDtypeStruct(s, jnp.float32) for s in outs],
            in_specs=[FARM if far_in else VM] * len(args),
            out_specs=[FARM if far_out else VM] * len(outs),
            scratch_shapes=[pltpu.VMEM(s, jnp.float32) if isinstance(s, tuple) else s for s in scratch],
            compiler_params=pltpu.CompilerParams(vmem_limit_bytes=16 * 2**20),
            cost_estimate=pl.CostEstimate(
                flops=int(us * 4e6), bytes_accessed=sum(4 * a.size for a in args), transcendentals=0
            ),
        )(*args)

    return run


def rows_of(k, n):
    return (k, n, *ROW)


def shifted(x, axis, by):
    count = lax.axis_size(axis)
    return lax.ppermute(x, axis, [(i, i + by) for i in range(count) if 0 <= i + by < count])


def both_ways(lows):
    return [p for i in lows for p in ((i, i + 1), (i + 1, i))]


def swapped(one, two):
    count = lax.axis_size(TM)
    return [
        lax.ppermute(x, TM, both_ways(range(start, count - 1, 2))) for x, start in ((one, 1), (two, 0))
    ]


def swapped_rows(x):
    cores, count = lax.axis_size(TM[-1]), lax.axis_size("lat")
    out = []
    for turn in range(2):
        lows = [
            core * count + i for core in range(cores) for i in range((core + turn + 1) % 2, count - 1, 2)
        ]
        out.append(lax.ppermute(x, (TM[-1], "lat"), both_ways(lows)))
    return out


def exchanged(x, axes):
    order = [0]
    for axis in axes:
        n = lax.axis_size(axis)
        order = [n * i + (k + n // 2) % n for i in order for k in range(n)]
    return lax.all_to_all(x, axes, 0, 0, axis_index_groups=[order], tiled=True)


def on_device(
    x_init, background, observed, diff_lon, diff_lat, drift, coupling, model_var, obs_level, huber_class
):
    band, wide = rows_of(L, ROWS), rows_of(L, W)
    whole = (L, ROWS, 8 * TILE)
    cells = (ROWS, *ROW)
    two_w = [wide] * 2
    count = float(L * ROWS * 8 * TILE * lax.axis_size(TM) * lax.axis_size("lat"))
    (own,) = call(
        pack_kernel,
        [rows_of(L + 3, ROWS)],
        [whole, (3, *whole[1:]), pltpu.SemaphoreType.DMA((4,))],
        far_in=True,
    )(x_init, diff_lon, diff_lat, drift)
    first, second = swapped_rows(own)
    x, bg, obs, c, keep, level, weight = call(
        aside_kernel, [band, band, cells, (L * L, *ROW), (L, *ROW), cells, cells]
    )(own, background, observed, coupling, model_var[None], obs_level, huber_class)
    after = shifted(x, TM, -1)
    inside_rows = rows_of(L, INNER)
    o1, inner = call(early_kernel, [cells, inside_rows], us=0.5)(c, own, obs, level, weight)
    first, second, bg, keep, o1, inner = lax.optimization_barrier(
        (first, second, bg, keep, o1, inner)
    )

    def half_way(factor):
        return call(
            lambda *refs: halo_kernel(factor, *refs), [band, band, inside_rows], [rows_of(L, 3 * H)] * 2
        )

    three = rows_of(L + 3, ROWS)
    up, down, moved, *sent = call(forward_kernel, [three, three, band, band, band], two_w)(
        c, first, second, own, inner
    )
    swaps = swapped(*sent)
    moved_halo, ahead_own, inner = half_way(0.5)(c, after, moved, up, own, down, up, own, down)
    *swaps, moved_halo = lax.optimization_barrier((*swaps, moved_halo))
    ahead, d, g = call(back_kernel, [wide, band, band], two_w)(
        c, *swaps, ahead_own, moved_halo, inner, up, own, down, bg, level, o1
    )

    first, second = swapped_rows(g)
    g0, g_copy, hg, inner, early = call(
        still_kernel, [band, band, cells, inside_rows, (2, *ROW)], two_w, 1.5
    )(c, keep, d, ahead, up, own, down, level, weight, o1, g)
    after_g = shifted(g_copy, TM, -1)
    first, second, g0 = lax.optimization_barrier((first, second, g0))
    up_g, down_g, moved_g, *sent = call(forward_g_kernel, [band] * 5, two_w)(
        c, first, second, g, up, own, down, inner
    )
    swaps = swapped(*sent)
    moved_halo, ahead_own, inner = half_way(1.0)(
        c, after_g, moved_g, up_g, g, down_g, up, own, down
    )
    *swaps, moved_halo = lax.optimization_barrier((*swaps, moved_halo))
    u, g1, part = call(
        back_g_kernel, [band, band, (lax.axis_size(NEAR), 1, TILE)], [wide] + two_w
    )(c, *swaps, ahead_own, moved_halo, inner, up, own, down, g, level, hg, g0, early)
    (part,) = call(again_kernel, [(lax.axis_size(FAR), 1, TILE)], us=0.1)(exchanged(part, NEAR))
    part = exchanged(part, FAR)

    def finish(*refs):
        last_kernel(count, *refs)

    outs = call(
        finish,
        [(1, *whole), (1, *whole), (1, *whole[1:])],
        [whole, whole, (1, *whole[1:]), pltpu.SemaphoreType.DMA((2 * L + 1,))],
        far_out=True,
    )(part, keep, own, g, g0, g1, d, u, o1, hg)
    return tuple(outs)


def solution(mesh):
    torus = Mesh(mesh.devices.reshape(4, 8, 2, mesh.shape["lat"]), (*TM, "lat"))
    band = P(TM, "lat", None)
    in_specs = (
        P(TM, None, "lat", None),
        P(None, "lat", None),
        band,
        band,
        band,
        band,
        P(),
        P(),
        band,
        band,
    )
    out_specs = (P(TM, None, "lat", None), P(TM, None, "lat", None), band)
    return jax.shard_map(
        on_device, mesh=torus, in_specs=in_specs, out_specs=out_specs, check_vma=False
    )
```
